512 devices in a mesh: dp: 128 (over z, y, core), mp: 4 (over x).
Axes of the slice: x: 4, y: 8, z: 8, core: 2. Of those that a mesh axis runs over, the one named last changes fastest.
Arguments:
- grad_out: bfloat16 [32768, 2304], P(('dp', 'mp')), may hold values from -6 to 6
- queries: bfloat16 [32768, 1536], P('dp', 'mp'), may hold values from -8 to 8
- keys: bfloat16 [4096, 1536], P('dp', 'mp'), may hold values from -8 to 8
- values: bfloat16 [4096, 1536], P('dp', 'mp'), may hold values from -6 to 6
- out_weight: bfloat16 [1536, 2304], P('mp'), may hold values from -0.15625 to 0.15625
- counts: int32 [128], P('dp'), may hold values from 0 to 4, as said below
- source: int32 [512], P('dp'), may hold values from 0 to 127, as said below
- offsets: int32 [512], P('dp'), may hold values from 0 to 16
- key_mask: int32 [512, 16], P('dp'), may hold values from 0 to 1, as said below
Outputs:
- query_grad: bfloat16 [32768, 1536], P('dp', 'mp')
- key_grad: bfloat16 [4096, 1536], P('dp', 'mp')
- value_grad: bfloat16 [4096, 1536], P('dp', 'mp')
- weight_grad: float32 [2304, 1536], P('dp', 'mp')
The draws below stay inside these ranges and needn't reach their ends.
Inputs may be any that keep to these rules, and one draw needn't show every extreme that they name: The live image slots of a rank are its first counts slots; the counts of all ranks sum to 128. `source`: the live image slots of all ranks name every rank exactly once; entries of slots that are not live are arbitrary. `key_mask`: the rows of an image's block that are not padding come first, and there are at least 8 of them.
All inputs are finite; a program needn't handle non-finite values.
Results may differ from the reference program's by a relative error of at most 0.04.
Values may be sent and summed in bfloat16 or wider, within the bound.
A program may use at most 64 MiB of HBM per device.

```python
import jax
import jax.numpy as jnp
from jax import lax

D = 2304
HEADS = 12
HEAD_DIM = 128
SLOTS = 4
PATCHES = 64
COND = 16
OWN_ROWS = 32
HH = 1536
IMAGES = 512
TOKENS = 32768
OWNED = 4096
N_DP = 128


def route_plan(key):
    key = jax.random.fold_in(key, 17)
    order_key, owner_key, spare_key = jax.random.split(key, 3)
    order = jax.random.permutation(order_key, N_DP)
    position = jnp.argsort(order).astype(jnp.int32)
    eighth = N_DP // 8
    counts = jnp.where(position < eighth, SLOTS, jnp.where(position < 2 * eighth, SLOTS // 2, jnp.where(position < 4 * eighth, 1, 0))).astype(jnp.int32)
    live = (jnp.arange(SLOTS)[None, :] < counts[:, None]).reshape(-1)
    live_rank = jnp.cumsum(live.astype(jnp.int32)) - 1
    owners = jax.random.permutation(owner_key, N_DP).astype(jnp.int32)
    filler = jax.random.randint(spare_key, (N_DP * SLOTS,), 0, N_DP)
    source = jnp.where(live, owners[jnp.clip(live_rank, 0, N_DP - 1)], filler).astype(jnp.int32)
    return (counts, source)


def draw_counts(key, part):
    plan = route_plan(key)
    return plan[0]


def draw_source(key, part):
    plan = route_plan(key)
    return plan[1]


def draw_key_mask(key, part):
    key = jax.random.fold_in(key, 11)
    lengths = jax.random.randint(key, (IMAGES,), COND // 2, COND + 1)
    lengths = jnp.where(jnp.arange(IMAGES) == 0, COND, lengths)
    return (jnp.arange(COND)[None, :] < lengths[:, None]).astype(jnp.int32)


def draw_queries(key, part):
    key = jax.random.fold_in(key, 3)
    shape = (TOKENS, HEADS, HEAD_DIM)
    field = jnp.clip(jax.random.normal(key, shape, jnp.float32), -8.0, 8.0)
    return field.reshape(TOKENS, HEADS * HEAD_DIM).astype(jnp.bfloat16)


def draw_keys(key, part):
    key = jax.random.fold_in(key, 5)
    shape = (OWNED, HEADS, HEAD_DIM)
    field = jnp.clip(jax.random.normal(key, shape, jnp.float32), -8.0, 8.0)
    return field.reshape(OWNED, HEADS * HEAD_DIM).astype(jnp.bfloat16)


def place_ends(drawn, key, least, high):
    longest = drawn.shape.index(max(drawn.shape))
    spots = []
    for shift in (0, 1):
        where = [jax.random.randint(jax.random.fold_in(key, axis), (), 0, length) for axis, length in enumerate(drawn.shape)]
        where[longest] = (where[longest] + shift) % drawn.shape[longest]
        spots.append(tuple(where))
    return drawn.at[spots[0]].set(least).at[spots[1]].set(high)


def shard_levels(own_key, extent, cuts, low, top_value):
    level, own = 1.0, jax.random.fold_in(own_key, 6)
    for dim, parts in cuts:
        draws = jnp.exp(jax.random.uniform(jax.random.fold_in(own, dim), (parts,), jnp.float32, low / len(cuts), top_value / len(cuts)))
        level = level * jnp.repeat(draws, extent[dim] // parts).reshape([-1 if axis == dim else 1 for axis in range(len(extent))])
    return level


def gaussian(stream_key, shape, spread, most, cuts=(), held_as=jnp.bfloat16):
    result = jax.random.normal(stream_key, shape, jnp.float32) * spread
    if len(cuts) > 0:
        result = shard_levels(stream_key, shape, cuts, -0.22, 0.18) * result
    return jnp.clip(result, min=-most, max=most).astype(held_as)


def setup_inputs(seed: int = 0) -> dict:
    streams_of = jax.random.split(jax.random.key(seed), 10)
    grad_out = gaussian(streams_of[0], (TOKENS, D), 1.0, 6.0, ((0, 512),))
    queries = draw_queries(jax.random.fold_in(streams_of[9], 71), 0)
    keys = draw_keys(jax.random.fold_in(streams_of[9], 71), 0)
    values = gaussian(streams_of[3], (OWNED, HH), 1.0, 6.0, ((0, 128), (1, 4)))
    out_weight = gaussian(streams_of[4], (HH, D), HH ** -0.5, 0.15625, ((0, 4),))
    counts = draw_counts(jax.random.fold_in(streams_of[9], 71), 0)
    source = draw_source(jax.random.fold_in(streams_of[9], 71), 0)
    offsets = place_ends(jax.random.randint(streams_of[7], (IMAGES,), 0, OWN_ROWS - COND + 1), jax.random.fold_in(streams_of[7], 1), 0, OWN_ROWS - COND).astype(jnp.int32)
    key_mask = draw_key_mask(jax.random.fold_in(streams_of[9], 71), 0)
    return dict(grad_out=grad_out, queries=queries, keys=keys, values=values, out_weight=out_weight, counts=counts, source=source, offsets=offsets, key_mask=key_mask)


def group_grads(pieces):
    query_blocks, key_blocks, value_blocks, grad_blocks, mask_blocks, live = pieces
    scale = HEAD_DIM ** -0.5
    query_wide = query_blocks.astype(jnp.float32)
    key_wide = key_blocks.astype(jnp.float32)
    value_wide = value_blocks.astype(jnp.float32)
    grad_wide = grad_blocks.astype(jnp.float32)
    scores = jnp.einsum('sqhd,skhd->shkq', query_wide, key_wide) * scale
    scores = jnp.where(mask_blocks[:, None, :, None] > 0, scores, -jnp.inf)
    highest = jnp.max(scores, axis=2, keepdims=True)
    expos = jnp.exp(scores - highest)
    probs = expos / jnp.sum(expos, axis=2, keepdims=True)
    probs_b = probs.astype(jnp.bfloat16)
    probs_wide = probs_b.astype(jnp.float32)
    live_four = live[:, None, None, None]
    attended = jnp.einsum('shkq,skhd->sqhd', probs_wide, value_wide)
    attended = jnp.where(live_four, attended, 0.0).astype(jnp.bfloat16)
    delta = jnp.sum(grad_wide * attended.astype(jnp.float32), axis=3)
    dprob = jnp.einsum('sqhd,skhd->shkq', grad_wide, value_wide)
    dscore = (probs * (dprob - jnp.transpose(delta, (0, 2, 1))[:, :, None, :])).astype(jnp.bfloat16)
    dscore_wide = dscore.astype(jnp.float32)
    query_grad = jnp.einsum('shkq,skhd->sqhd', dscore_wide, key_wide) * scale
    query_grad = jnp.where(live_four, query_grad, 0.0).astype(jnp.bfloat16)
    key_part = jnp.einsum('shkq,sqhd->skhd', dscore_wide, query_wide) * scale
    key_part = jnp.where(live_four, key_part, 0.0).astype(jnp.bfloat16)
    value_part = jnp.einsum('shkq,sqhd->skhd', probs_wide, grad_wide)
    value_part = jnp.where(live_four, value_part, 0.0).astype(jnp.bfloat16)
    return attended, query_grad, key_part, value_part


def reference(grad_out, queries, keys, values, out_weight, counts, source, offsets, key_mask):
    grad_attn = jnp.dot(grad_out, out_weight.T, preferred_element_type=jnp.float32).astype(jnp.bfloat16)
    live = jnp.arange(SLOTS)[None, :] < counts[:, None]
    row_ids = (source.reshape(N_DP, SLOTS)[:, :, None] * OWN_ROWS + offsets.reshape(N_DP, SLOTS)[:, :, None]
               + jnp.arange(COND)[None, None, :]).astype(jnp.int32)
    flat_rows = row_ids.reshape(-1)
    key_blocks = jnp.take(keys, flat_rows, axis=0).reshape(N_DP, SLOTS, COND, HEADS, HEAD_DIM)
    value_blocks = jnp.take(values, flat_rows, axis=0).reshape(N_DP, SLOTS, COND, HEADS, HEAD_DIM)
    query_blocks = queries.reshape(N_DP, SLOTS, PATCHES, HEADS, HEAD_DIM)
    grad_blocks = grad_attn.reshape(N_DP, SLOTS, PATCHES, HEADS, HEAD_DIM)
    mask_blocks = key_mask.reshape(N_DP, SLOTS, COND)
    attended, query_grad, key_part, value_part = lax.map(
        group_grads, (query_blocks, key_blocks, value_blocks, grad_blocks, mask_blocks, live))
    attended_rows = attended.reshape(TOKENS, HH)
    weight_grad = jnp.dot(grad_out.T, attended_rows, preferred_element_type=jnp.float32)
    key_grad = jnp.zeros((OWNED, HH), jnp.float32).at[flat_rows].add(
        key_part.reshape(-1, HH).astype(jnp.float32)).astype(jnp.bfloat16)
    value_grad = jnp.zeros((OWNED, HH), jnp.float32).at[flat_rows].add(
        value_part.reshape(-1, HH).astype(jnp.float32)).astype(jnp.bfloat16)
    return query_grad.reshape(TOKENS, HH), key_grad, value_grad, weight_grad
```

```python
import functools

import jax
import jax.numpy as jnp
from jax import lax
from jax.experimental import pallas as pl
from jax.experimental.pallas import tpu as pltpu
from jax.sharding import PartitionSpec as P

HEAD_DIM = 128
NZ, NY, NC, NX = 8, 8, 2, 4
MESH = pl.DeviceIdType.MESH
F32, BF16, I32 = jnp.float32, jnp.bfloat16, jnp.int32
NN = (((1,), (0,)), ((), ()))
NT = (((1,), (1,)), ((), ()))
TN = (((0,), (0,)), ((), ()))


def dot(a, b, dims):
    return lax.dot_general(a, b, dims, preferred_element_type=F32)


def total(ref, slots):
    acc = ref[0].astype(F32)
    for i in range(1, slots):
        acc = acc + ref[i].astype(F32)
    return acc


def kernel(
    counts, source, offsets, mask, g_hbm, q_hbm, k_hbm, v_hbm, w_hbm,
    qg_out, kg_out, vg_out, wg_out,
    q_v, w_v, g_all, g_other, gt,
    k_rows, v_rows, meta_z, meta_y, pick_k, pick_v,
    k_sel, v_sel, k_in, v_in,
    att, att_other, k_back, v_back, k_spread, v_spread, k_other, v_other,
    k_send, v_send, k_last, v_last,
    w_part, w_send, w_in, w_pad, w_last,
    local_sem, pair_send, pair_recv, x_send, x_recv, z_send, z_recv, y_send, y_recv,
):
    scale = HEAD_DIM ** -0.5
    dp, x = lax.axis_index("dp"), lax.axis_index("mp")
    z, y, c = lax.div(dp, NY * NC), lax.rem(lax.div(dp, NC), NY), lax.rem(dp, NC)
    slots, patches, cond, own = 4, 64, 16, 32
    width = q_v.shape[1]
    heads = width // HEAD_DIM

    def place(z, y, c, x):
        return ((z * NY + y) * NC + c, x)

    z_at = [lax.rem(z + k, NZ) for k in range(NZ)]
    y_at = [lax.rem(y + k, NY) for k in range(NY)]
    z_peer = [place(z_at[k], y, c, x) for k in range(NZ)]
    y_peer = [place(z, y_at[k], c, x) for k in range(NY)]
    x_peer = [place(z, y, c, lax.rem(x + k, NX)) for k in range(NX)]
    pair = place(z, y, 1 - c, x)

    started = []

    def push(src, dst, send, recv, device):
        copy = pltpu.make_async_remote_copy(
            src_ref=src, dst_ref=dst, send_sem=send, recv_sem=recv,
            device_id=device, device_id_type=MESH,
        )
        copy.start()
        started.append(copy)
        return copy

    def along_z(line, source_of, dst):
        return [
            push(source_of(k), dst.at[z], z_send.at[line, k], z_recv.at[line, k], z_peer[k])
            for k in range(1, NZ)
        ]

    def along_y(line, source_of, dst):
        return [
            push(source_of(k), dst.at[y], y_send.at[line, k], y_recv.at[line, k], y_peer[k])
            for k in range(1, NY)
        ]

    def across(line, src, dst):
        return push(src, dst, pair_send.at[line], pair_recv.at[line], pair)

    def arrive(copies):
        for copy in copies:
            copy.wait_recv()

    def load(i, src, dst):
        copy = pltpu.make_async_copy(src, dst, local_sem.at[i])
        copy.start()
        return copy

    load_k = load(0, k_hbm, k_rows.at[c, y])
    load_v = load(1, v_hbm, v_rows.at[c, z])
    load_g = load(2, g_hbm, g_all.at[x])
    load_q = load(3, q_hbm, q_v)
    load_w = load(4, w_hbm, w_v)

    lane = lax.broadcasted_iota(I32, (8, 128), 1)
    slot, row = (lane >> 4) & 3, lane & 15
    rows_named = jnp.full((8, 128), -(1 << 20), I32)
    for j in range(slots):
        first = jnp.where(j < counts[0], source[j] * own + offsets[j], -(1 << 20))
        rows_named = jnp.where(slot == j, first + row, rows_named)
    meta_z[z] = rows_named
    meta_y[y] = rows_named

    barrier = pltpu.get_barrier_semaphore()
    for device in [pair] + x_peer[1:] + z_peer[1:] + y_peer[1:]:
        pl.semaphore_signal(barrier, inc=1, device_id=device, device_id_type=MESH)
    pl.semaphore_wait(barrier, 1 + (NX - 1) + (NZ - 1) + (NY - 1))

    k_rows_sent = along_y(0, lambda k: k_hbm, k_rows.at[c])
    v_rows_sent = along_z(0, lambda k: v_hbm, v_rows.at[c])
    x_sent = [
        push(g_hbm, g_all.at[x], x_send.at[k], x_recv.at[k], x_peer[k]) for k in range(1, NX)
    ]
    meta_z_sent = along_z(1, lambda k: meta_z.at[z], meta_z)
    meta_y_sent = along_y(1, lambda k: meta_y.at[y], meta_y)
    g_pair = [across(0, g_hbm, g_other.at[x])]

    arrive(meta_z_sent)
    arrive(meta_y_sent)
    in_first = lax.broadcasted_iota(I32, (1, 128), 1) < 64
    rows_of = lax.broadcasted_iota(I32, (NC * NZ * own, 128), 0)

    def one_hot(meta, along, keep, pick):
        for p in range(4):
            ids = jnp.where(in_first, meta[2 * p, 0:1, :], meta[2 * p + 1, 0:1, :])
            local = ((ids >> 5) & 1) * (8 * own) + along(ids) * own + (ids & (own - 1))
            local = jnp.where(keep(ids), local, -1)
            pick[:, 128 * p : 128 * (p + 1)] = jnp.where(rows_of == local, 1.0, 0.0).astype(BF16)

    one_hot(meta_z, lambda i: (i >> 6) & 7, lambda i: (i >> 9) == z, pick_k)
    one_hot(meta_y, lambda i: i >> 9, lambda i: (i >= 0) & (((i >> 6) & 7) == y), pick_v)

    load_k.wait()
    arrive(k_rows_sent)
    k_pair = across(1, k_rows.at[c], k_rows.at[c])
    load_v.wait()
    arrive(v_rows_sent)
    v_pair = across(2, v_rows.at[c], v_rows.at[c])

    k_pair.wait_recv()
    k_sel[...] = (
        dot(pick_k[...], k_rows[...].reshape(512, width), TN).astype(BF16).reshape(8, 64, width)
    )
    k_in_sent = along_z(2, lambda k: k_sel.at[z_at[k]], k_in)
    k_in[z] = k_sel[z]
    v_pair.wait_recv()
    v_sel[...] = (
        dot(pick_v[...], v_rows[...].reshape(512, width), TN).astype(BF16).reshape(8, 64, width)
    )
    v_in_sent = along_y(2, lambda k: v_sel.at[y_at[k]], v_in)
    v_in[y] = v_sel[y]

    for k in range(1, NX):
        x_sent[k - 1].wait_recv()
        came = lax.rem(x + NX - k, NX)
        g_pair.append(across(2 + k, g_all.at[came], g_other.at[came]))
    load_g.wait()
    load_w.wait()
    load_q.wait()
    g = g_all[...].reshape(slots * patches, -1)
    ga = dot(g, w_v[...], NT).astype(BF16)
    gt[:, 0:256] = g.T
    arrive(g_pair)
    gt[:, 256:512] = g_other[...].reshape(slots * patches, -1).T

    eye = lax.broadcasted_iota(I32, (cond, cond), 0) == lax.broadcasted_iota(I32, (cond, cond), 1)
    kept = jnp.concatenate(
        [
            jnp.sum(jnp.where(eye, mask[s : s + 1, :].astype(F32), 0.0), axis=1, keepdims=True)
            for s in range(slots)
        ],
        axis=0,
    )
    same_slot = (lax.broadcasted_iota(I32, (64, 256), 0) >> 4) == (
        lax.broadcasted_iota(I32, (64, 256), 1) >> 6
    )

    def grouped(a, op):
        a = a.reshape(slots, cond, 256)
        a = op(a, axis=1, keepdims=True)
        return jnp.broadcast_to(a, (slots, cond, 256)).reshape(64, 256)

    arrive(k_in_sent)
    k_blocks = total(k_in, NZ).astype(BF16)
    q = q_v[...]
    probs = []
    for h in range(heads):
        cols = slice(h * HEAD_DIM, (h + 1) * HEAD_DIM)
        scores = dot(k_blocks[:, cols], q[:, cols], NT) * scale
        scores = jnp.where(kept > 0.5, scores, -1e30)
        expos = jnp.exp(scores - grouped(scores, jnp.max))
        probs.append(jnp.where(same_slot, expos / grouped(expos, jnp.sum), 0.0))
    arrive(v_in_sent)
    v_blocks = total(v_in, NY).astype(BF16)
    for h in range(heads):
        cols = slice(h * HEAD_DIM, (h + 1) * HEAD_DIM)
        att[:, cols] = dot(probs[h].astype(BF16), v_blocks[:, cols], TN).astype(BF16)
    att_pair = across(6, att, att_other)

    dscores = []
    for h in range(heads):
        cols = slice(h * HEAD_DIM, (h + 1) * HEAD_DIM)
        probs_b = probs[h].astype(BF16)
        dprob = dot(v_blocks[:, cols], ga[:, cols], NT)
        delta = grouped(probs_b.astype(F32) * dprob, jnp.sum)
        dscore = (probs[h] * (dprob - delta)).astype(BF16)
        dscores.append(dscore)
        k_back[z, :, cols] = (dot(dscore, q[:, cols], NN) * scale).astype(BF16)
        v_back[y, :, cols] = dot(probs_b, ga[:, cols], NN).astype(BF16)
    k_back_sent = along_z(3, lambda k: k_back.at[z], k_back)
    v_back_sent = along_y(3, lambda k: v_back.at[y], v_back)

    att_pair.wait_recv()
    for b in range(6):
        rows = slice(b * 384, (b + 1) * 384)
        part = dot(gt[rows, 0:256], att[...], NN) + dot(gt[rows, 256:512], att_other[...], NN)
        w_part[rows, :] = part.astype(BF16)
    i = lax.broadcasted_iota(I32, (144, 288), 0)
    parity = jnp.where(
        lax.broadcasted_iota(I32, (144, 288), 1) == i + 18 * ((i * 3641) >> 16) + 18 * c, 1.0, 0.0
    ).astype(BF16)
    for b in range(NZ):
        w_send[b] = dot(parity, w_part[b * 288 : (b + 1) * 288, :], NN).astype(BF16)
    w_sent = along_z(4, lambda k: w_send.at[z_at[k]], w_in)
    w_in[z] = w_send[z]

    for h in range(heads):
        cols = slice(h * HEAD_DIM, (h + 1) * HEAD_DIM)
        qg_out[:, cols] = (dot(dscores[h], k_blocks[:, cols], TN) * scale).astype(BF16)

    arrive(k_back_sent)
    k_spread[...] = (
        dot(pick_k[...], k_back[...].reshape(512, width), NN).astype(BF16).reshape(2, 8, own, width)
    )
    k_swap = across(7, k_spread.at[1 - c], k_other)
    arrive(v_back_sent)
    v_spread[...] = (
        dot(pick_v[...], v_back[...].reshape(512, width), NN).astype(BF16).reshape(2, 8, own, width)
    )
    v_swap = across(8, v_spread.at[1 - c], v_other)
    k_swap.wait_recv()
    k_send[...] = k_spread[c] + k_other[...]
    k_last_sent = along_y(4, lambda k: k_send.at[y_at[k]], k_last)
    k_last[y] = k_send[y]
    v_swap.wait_recv()
    v_send[...] = v_spread[c] + v_other[...]
    v_last_sent = along_z(5, lambda k: v_send.at[z_at[k]], v_last)
    v_last[z] = v_send[z]

    arrive(w_sent)
    summed = total(w_in, NZ).astype(BF16)
    o = lax.broadcasted_iota(I32, (256, 144), 0)
    spread = jnp.where(
        ((o & 31) < 18) & (lax.broadcasted_iota(I32, (256, 144), 1) == (o >> 5) * 18 + (o & 31)),
        1.0, 0.0,
    ).astype(BF16)
    w_pad[...] = dot(spread, summed, NN).astype(BF16).reshape(8, 32, width)
    w_last_sent = along_y(5, lambda k: w_pad.at[y_at[k]], w_last)
    w_last[y] = w_pad[y]

    arrive(k_last_sent)
    kg_out[...] = total(k_last, NY).astype(BF16)
    arrive(v_last_sent)
    vg_out[...] = total(v_last, NZ).astype(BF16)
    arrive(w_last_sent)
    wg_out[...] = total(w_last, NY)[0:18, :]
    for copy in started:
        copy.wait_send()


def on_device(grad_out, queries, keys, values, out_weight, counts, source, offsets, key_mask):
    patches, d = grad_out.shape
    tokens, width = queries.shape
    own = keys.shape[0]
    vmem = lambda *shape, dtype=BF16: pltpu.VMEM(shape, dtype)
    smem = pl.BlockSpec(memory_space=pltpu.SMEM)
    whole = pl.BlockSpec(memory_space=pltpu.VMEM)
    hbm = pl.BlockSpec(memory_space=pl.ANY)
    dma = lambda *shape: pltpu.SemaphoreType.DMA(shape)
    return pl.pallas_call(
        kernel,
        out_shape=(
            jax.ShapeDtypeStruct((tokens, width), BF16),
            jax.ShapeDtypeStruct((own, width), BF16),
            jax.ShapeDtypeStruct((own, width), BF16),
            jax.ShapeDtypeStruct((d // (NZ * NY * NC), width), F32),
        ),
        in_specs=[smem, smem, smem, whole, hbm, hbm, hbm, hbm, hbm],
        out_specs=(whole,) * 4,
        scratch_shapes=[
            vmem(tokens, width), vmem(width, d), vmem(NX, patches, d), vmem(NX, patches, d),
            vmem(d, 512),
            vmem(NC, NY, own, width), vmem(NC, NZ, own, width),
            vmem(NZ, 8, 128, dtype=I32), vmem(NY, 8, 128, dtype=I32),
            vmem(512, 512), vmem(512, 512),
            vmem(NZ, 64, width), vmem(NY, 64, width), vmem(NZ, 64, width), vmem(NY, 64, width),
            vmem(tokens, width), vmem(tokens, width), vmem(NZ, 64, width), vmem(NY, 64, width),
            vmem(NC, NY, own, width), vmem(NC, NZ, own, width),
            vmem(NY, own, width), vmem(NZ, own, width),
            vmem(NY, own, width), vmem(NZ, own, width), vmem(NY, own, width), vmem(NZ, own, width),
            vmem(d, width), vmem(NZ, 144, width), vmem(NZ, 144, width),
            vmem(NY, 32, width), vmem(NY, 32, width),
            dma(5), dma(9), dma(9), dma(NX), dma(NX),
            dma(6, NZ), dma(6, NZ), dma(6, NY), dma(6, NY),
        ],
        compiler_params=pltpu.CompilerParams(
            collective_id=0, has_side_effects=True, vmem_limit_bytes=48 << 20
        ),
        name="routed_attention_backward",
    )(counts, source, offsets, key_mask, grad_out, queries, keys, values, out_weight)


def solution(mesh):
    in_specs = (
        P(("dp", "mp"), None),
        P("dp", "mp"),
        P("dp", "mp"),
        P("dp", "mp"),
        P("mp", None),
        P("dp"),
        P("dp"),
        P("dp"),
        P("dp", None),
    )
    out_specs = (P("dp", "mp"), P("dp", "mp"), P("dp", "mp"), P("dp", "mp"))
    return jax.shard_map(
        on_device, mesh=mesh, in_specs=in_specs, out_specs=out_specs, check_vma=False
    )
```

```python
import functools

import jax
import jax.numpy as jnp
from jax import lax
from jax.experimental import pallas as pl
from jax.experimental.pallas import tpu as pltpu
from jax.sharding import PartitionSpec as P

HEAD_DIM = 128
NZ, NY, NC, NX = 8, 8, 2, 4
MESH = pl.DeviceIdType.MESH
F32, BF16, I32 = jnp.float32, jnp.bfloat16, jnp.int32
NN = (((1,), (0,)), ((), ()))
NT = (((1,), (1,)), ((), ()))
TN = (((0,), (0,)), ((), ()))


def dot(a, b, dims):
    return lax.dot_general(a, b, dims, preferred_element_type=F32)


def total(ref, slots):
    acc = ref[0].astype(F32)
    for i in range(1, slots):
        acc = acc + ref[i].astype(F32)
    return acc


def kernel(
    counts, source_h, offsets_h, mask_h, g_h, q_h, k_h, v_h, w_h,
    qg_out, kg_out, vg_out, wg_out,
    source, offsets, mask, q_v, w_v, g_all, g_other, gt,
    kv_own, rows, meta_own, meta, pick, sel, kv_in,
    att, att_other, back_own, back, spread, last,
    w_part, w_turn, w_turned, wz_send, wy_send, wz_in, wy_in, wz_pad, wy_pad, wz_last, wy_last,
    local_sem, pair_send, pair_recv, x_send, x_recv, send, recv, w_sent, w_recv,
):
    scale = HEAD_DIM ** -0.5
    dp, x = lax.axis_index("dp"), lax.axis_index("mp")
    z, y, c = lax.div(dp, NY * NC), lax.rem(lax.div(dp, NC), NY), lax.rem(dp, NC)
    slots, patches, cond, own = 4, 64, 16, 32
    width = q_v.shape[1]
    heads = width // HEAD_DIM

    def place(z, y, c):
        return ((z * NY + y) * NC + c, x)

    z_at = [lax.rem(z + k, NZ) for k in range(NZ)]
    y_at = [lax.rem(y + k, NY) for k in range(NY)]
    from_at = [jnp.where(c == 0, y_at[k], z_at[k]) for k in range(8)]
    to_at = [jnp.where(c == 0, z_at[k], y_at[k]) for k in range(8)]
    pair = place(z, y, 1 - c)
    x_peer = [((z * NY + y) * NC + c, lax.rem(x + k, NX)) for k in range(NX)]

    def on_z(k, core):
        return place(z_at[k], y, core)

    def on_y(k, core):
        return place(z, y_at[k], core)

    def on_from(k, core):
        return place(jnp.where(c == 0, z, z_at[k]), jnp.where(c == 0, y_at[k], y), core)

    def on_to(k, core):
        return place(jnp.where(c == 0, z_at[k], z), jnp.where(c == 0, y, y_at[k]), core)

    started = []

    def push(src, dst, sent, got, device):
        copy = pltpu.make_async_remote_copy(
            src_ref=src, dst_ref=dst, send_sem=sent, recv_sem=got,
            device_id=device, device_id_type=MESH,
        )
        copy.start()
        started.append(copy)
        return copy

    def expect(dst, got):
        pltpu.make_async_remote_copy(
            src_ref=dst, dst_ref=dst, send_sem=pair_send.at[0], recv_sem=got,
            device_id=pair, device_id_type=MESH,
        ).wait_recv()

    def load(i, src, dst):
        copy = pltpu.make_async_copy(src, dst, local_sem.at[i])
        copy.start()
        return copy

    int_loads = [load(1, source_h, source), load(2, offsets_h, offsets)]
    load_k = load(3, k_h, kv_own.at[0])
    load_v = load(4, v_h, kv_own.at[1])
    load_g = load(5, g_h, g_all.at[x])
    load_m = load(6, mask_h, mask)
    load_q = load(7, q_h, q_v)
    load_w = load(8, w_h, w_v)

    barrier = pltpu.get_barrier_semaphore()
    near = [pair] + x_peer[1:]
    for core in range(NC):
        near += [on_z(k, core) for k in range(1, NZ)] + [on_y(k, core) for k in range(1, NY)]
    for device in near:
        pl.semaphore_signal(barrier, inc=1, device_id=device, device_id_type=MESH)

    for copy in int_loads:
        copy.wait()
    lane = lax.broadcasted_iota(I32, (8, 128), 1)
    slot, row = (lane >> 4) & 3, lane & 15
    named = jnp.full((8, 128), -(1 << 20), I32)
    for j in range(slots):
        first = jnp.where(j < counts[0], source[j] * own + offsets[j], -(1 << 20))
        named = jnp.where(slot == j, first + row, named)
    meta_own[...] = named
    meta[to_at[0], c] = named
    load_k.wait()
    load_v.wait()
    rows[from_at[0], c] = kv_own[c]
    load_g.wait()
    pl.semaphore_wait(barrier, len(near))

    for k in range(1, 8):
        push(kv_own.at[0], rows.at[y, c], send.at[0, 0, k], recv.at[0, c, k], on_y(k, 0))
        push(kv_own.at[1], rows.at[z, c], send.at[0, 1, k], recv.at[0, c, k], on_z(k, 1))
    push(kv_own.at[1 - c], rows.at[to_at[0], c], send.at[0, 0, 0], recv.at[0, c, 0], pair)
    for k in range(1, 8):
        push(meta_own, meta.at[z, c], send.at[1, 0, k], recv.at[1, c, k], on_z(k, 0))
        push(meta_own, meta.at[y, c], send.at[1, 1, k], recv.at[1, c, k], on_y(k, 1))
    push(meta_own, meta.at[from_at[0], c], send.at[1, 0, 0], recv.at[1, c, 0], pair)
    x_sent = [
        push(g_all.at[x], g_all.at[x], x_send.at[k], x_recv.at[k], x_peer[k]) for k in range(1, NX)
    ]
    g_pair = [push(g_all.at[x], g_other.at[x], pair_send.at[0], pair_recv.at[0], pair)]

    def arrive(line, dst):
        for k in range(1, 8):
            for core in range(NC):
                expect(dst, recv.at[line, core, k])
        expect(dst, recv.at[line, 1 - c, 0])

    def arrive_w(line, dst):
        for k in range(1, 8):
            expect(dst, w_recv.at[line, k])

    arrive(1, meta_own)
    left = lax.broadcasted_iota(I32, (1, 128), 1) < 64
    rows_of = lax.broadcasted_iota(I32, (512, 128), 0)
    for p in range(8):
        ids = jnp.where(left, meta[p, 0, 0:1, :], meta[p, 1, 0:1, :])
        ids_z, ids_y = ids >> 9, (ids >> 6) & 7
        keep = (ids >= 0) & (jnp.where(c == 0, ids_z, ids_y) == to_at[0])
        local = jnp.where(keep, jnp.where(c == 0, ids_y, ids_z) * 64 + (ids & 63), -1)
        pick[:, 128 * p : 128 * (p + 1)] = jnp.where(rows_of == local, 1.0, 0.0).astype(BF16)

    arrive(0, kv_own.at[0])
    sel[...] = (
        dot(pick[...], rows[...].reshape(512, width), TN).astype(BF16).reshape(8, 2, 64, width)
    )
    for k in range(1, 8):
        for core in range(NC):
            push(
                sel.at[to_at[k], core], kv_in.at[c, to_at[0]],
                send.at[2, core, k], recv.at[2, c, k], on_to(k, core),
            )
    push(
        sel.at[to_at[0], 1 - c], kv_in.at[c, to_at[0]],
        send.at[2, 0, 0], recv.at[2, c, 0], pair,
    )
    kv_in[c, to_at[0]] = sel[to_at[0], c]

    for k in range(1, NX):
        x_sent[k - 1].wait_recv()
        came = lax.rem(x + NX - k, NX)
        g_pair.append(
            push(g_all.at[came], g_other.at[came], pair_send.at[k], pair_recv.at[k], pair)
        )
    load_w.wait()
    load_q.wait()
    load_m.wait()
    g = g_all[...].reshape(slots * patches, -1)
    ga = dot(g, w_v[...], NT).astype(BF16)
    gt[:, 0:256] = g.T
    for copy in g_pair:
        copy.wait_recv()
    gt[:, 256:512] = g_other[...].reshape(slots * patches, -1).T

    eye = lax.broadcasted_iota(I32, (cond, cond), 0) == lax.broadcasted_iota(I32, (cond, cond), 1)
    kept = jnp.concatenate(
        [
            jnp.sum(jnp.where(eye, mask[s : s + 1, :].astype(F32), 0.0), axis=1, keepdims=True)
            for s in range(slots)
        ],
        axis=0,
    )
    same_slot = (lax.broadcasted_iota(I32, (64, 256), 0) >> 4) == (
        lax.broadcasted_iota(I32, (64, 256), 1) >> 6
    )

    def grouped(a, op):
        a = a.reshape(slots, cond, 256)
        a = op(a, axis=1, keepdims=True)
        return jnp.broadcast_to(a, (slots, cond, 256)).reshape(64, 256)

    arrive(2, kv_in.at[0, 0])
    k_blocks = total(kv_in.at[0], 8).astype(BF16)
    v_blocks = total(kv_in.at[1], 8).astype(BF16)
    q = q_v[...]
    probs = []
    for h in range(heads):
        cols = slice(h * HEAD_DIM, (h + 1) * HEAD_DIM)
        scores = dot(k_blocks[:, cols], q[:, cols], NT) * scale
        scores = jnp.where(kept > 0.5, scores, -1e30)
        expos = jnp.exp(scores - grouped(scores, jnp.max))
        probs.append(jnp.where(same_slot, expos / grouped(expos, jnp.sum), 0.0))
        att[:, cols] = dot(probs[h].astype(BF16), v_blocks[:, cols], TN).astype(BF16)
    att_pair = push(att, att_other, pair_send.at[4], pair_recv.at[4], pair)

    dscores = []
    for h in range(heads):
        cols = slice(h * HEAD_DIM, (h + 1) * HEAD_DIM)
        probs_b = probs[h].astype(BF16)
        dprob = dot(v_blocks[:, cols], ga[:, cols], NT)
        delta = grouped(probs_b.astype(F32) * dprob, jnp.sum)
        dscore = (probs[h] * (dprob - delta)).astype(BF16)
        dscores.append(dscore)
        back_own[0, :, cols] = (dot(dscore, q[:, cols], NN) * scale).astype(BF16)
        back_own[1, :, cols] = dot(probs_b, ga[:, cols], NN).astype(BF16)
    for k in range(1, 8):
        push(back_own.at[0], back.at[z, c], send.at[3, 0, k], recv.at[3, c, k], on_z(k, 0))
        push(back_own.at[1], back.at[y, c], send.at[3, 1, k], recv.at[3, c, k], on_y(k, 1))
    push(back_own.at[1 - c], back.at[from_at[0], c], send.at[3, 0, 0], recv.at[3, c, 0], pair)
    back[to_at[0], c] = back_own[c]

    att_pair.wait_recv()
    for b in range(6):
        part = slice(b * 384, (b + 1) * 384)
        w_part[part, :] = (
            dot(gt[part, 0:256], att[...], NN) + dot(gt[part, 256:512], att_other[...], NN)
        ).astype(BF16)
    i = lax.broadcasted_iota(I32, (144, 288), 0)
    parity = jnp.where(
        lax.broadcasted_iota(I32, (144, 288), 1) == i + 18 * ((i * 3641) >> 16) + 18 * c, 1.0, 0.0
    ).astype(BF16)
    for b in range(NZ):
        part = dot(parity, w_part[b * 288 : (b + 1) * 288, :], NN)
        wz_send[b] = part[:, 0:256].astype(BF16)
        w_turn[b] = part[:, 256:384]
    wz_in[z] = wz_send[z]
    for k in range(1, NZ):
        push(wz_send.at[z_at[k]], wz_in.at[z], w_sent.at[0, k], w_recv.at[0, k], on_z(k, c))
    for b in range(NZ):
        for a in range(NY):
            w_turned[a, b * 18 : (b + 1) * 18, :] = w_turn[b, a * 18 : (a + 1) * 18, :]
    wy_send[...] = w_turned[...].astype(BF16)
    wy_in[y] = wy_send[y]
    for k in range(1, NY):
        push(wy_send.at[y_at[k]], wy_in.at[y], w_sent.at[1, k], w_recv.at[1, k], on_y(k, c))

    for h in range(heads):
        cols = slice(h * HEAD_DIM, (h + 1) * HEAD_DIM)
        qg_out[:, cols] = (dot(dscores[h], k_blocks[:, cols], TN) * scale).astype(BF16)

    arrive(3, back_own.at[0])
    spread[...] = (
        dot(pick[...], back[...].reshape(1024, width), NN).astype(BF16).reshape(8, 2, own, width)
    )
    for k in range(1, 8):
        for core in range(NC):
            push(
                spread.at[from_at[k], core], last.at[c, from_at[0]],
                send.at[4, core, k], recv.at[4, c, k], on_from(k, core),
            )
    push(
        spread.at[from_at[0], 1 - c], last.at[c, from_at[0]],
        send.at[4, 0, 0], recv.at[4, c, 0], pair,
    )
    last[c, from_at[0]] = spread[from_at[0], c]

    o = lax.broadcasted_iota(I32, (256, 144), 0)
    pad = jnp.where(
        ((o & 31) < 18) & (lax.broadcasted_iota(I32, (256, 144), 1) == (o >> 5) * 18 + (o & 31)),
        1.0, 0.0,
    ).astype(BF16)
    arrive_w(1, wy_in.at[0])
    wy_pad[...] = dot(pad, total(wy_in, NY).astype(BF16), NN).astype(BF16).reshape(8, 32, 128)
    wy_last[z] = wy_pad[z]
    for k in range(1, NZ):
        push(wy_pad.at[z_at[k]], wy_last.at[z], w_sent.at[2, k], w_recv.at[2, k], on_z(k, c))
    arrive_w(0, wz_in.at[0])
    wz_pad[...] = dot(pad, total(wz_in, NZ).astype(BF16), NN).astype(BF16).reshape(8, 32, 256)
    wz_last[y] = wz_pad[y]
    for k in range(1, NY):
        push(wz_pad.at[y_at[k]], wz_last.at[y], w_sent.at[3, k], w_recv.at[3, k], on_y(k, c))

    arrive(4, last.at[0, 0])
    kg_out[...] = total(last.at[0], 8).astype(BF16)
    vg_out[...] = total(last.at[1], 8).astype(BF16)
    arrive_w(2, wy_last.at[0])
    wg_out[:, 256:384] = total(wy_last, NZ)[0:18, :]
    arrive_w(3, wz_last.at[0])
    wg_out[:, 0:256] = total(wz_last, NY)[0:18, :]
    for copy in started:
        copy.wait_send()


def on_device(grad_out, queries, keys, values, out_weight, counts, source, offsets, key_mask):
    patches, d = grad_out.shape
    tokens, width = queries.shape
    own = keys.shape[0]
    slots, cond = key_mask.shape
    vmem = lambda *shape, dtype=BF16: pltpu.VMEM(shape, dtype)
    whole = pl.BlockSpec(memory_space=pltpu.VMEM)
    hbm = pl.BlockSpec(memory_space=pltpu.HBM)
    dma = lambda *shape: pltpu.SemaphoreType.DMA(shape)
    operands = (source, offsets, key_mask, grad_out, queries, keys, values, out_weight)
    operands = [pltpu.with_memory_space_constraint(a, pltpu.HBM) for a in operands]
    return pl.pallas_call(
        kernel,
        out_shape=(
            jax.ShapeDtypeStruct((tokens, width), BF16),
            jax.ShapeDtypeStruct((own, width), BF16),
            jax.ShapeDtypeStruct((own, width), BF16),
            jax.ShapeDtypeStruct((d // (NZ * NY * NC), width), F32),
        ),
        in_specs=[pl.BlockSpec(memory_space=pltpu.SMEM)] + [hbm] * 8,
        out_specs=(whole,) * 4,
        scratch_shapes=[
            pltpu.SMEM((slots,), I32), pltpu.SMEM((slots,), I32),
            vmem(slots, cond, dtype=I32),
            vmem(tokens, width), vmem(width, d), vmem(NX, patches, d), vmem(NX, patches, d),
            vmem(d, 512),
            vmem(2, own, width), vmem(8, NC, own, width),
            vmem(8, 128, dtype=I32), vmem(8, NC, 8, 128, dtype=I32),
            vmem(512, 1024), vmem(8, NC, 64, width), vmem(2, 8, 64, width),
            vmem(tokens, width), vmem(tokens, width),
            vmem(2, 64, width), vmem(8, NC, 64, width),
            vmem(8, NC, own, width), vmem(2, 8, own, width),
            vmem(d, width), vmem(NZ, 144, 128, dtype=F32), vmem(NY, 144, 128, dtype=F32),
            vmem(NZ, 144, 256), vmem(NY, 144, 128), vmem(NZ, 144, 256), vmem(NY, 144, 128),
            vmem(NY, 32, 256), vmem(NZ, 32, 128), vmem(NY, 32, 256), vmem(NZ, 32, 128),
            dma(9), dma(5), dma(5), dma(NX), dma(NX),
            dma(5, 2, 8), dma(5, 2, 8), dma(4, 8), dma(4, 8),
        ],
        compiler_params=pltpu.CompilerParams(
            collective_id=0, has_side_effects=True, vmem_limit_bytes=48 << 20
        ),
        name="routed_attention_backward",
    )(counts, *operands)


def solution(mesh):
    in_specs = (
        P(("dp", "mp"), None),
        P("dp", "mp"),
        P("dp", "mp"),
        P("dp", "mp"),
        P("mp", None),
        P("dp"),
        P("dp"),
        P("dp"),
        P("dp", None),
    )
    out_specs = (P("dp", "mp"), P("dp", "mp"), P("dp", "mp"), P("dp", "mp"))
    return jax.shard_map(
        on_device, mesh=mesh, in_specs=in_specs, out_specs=out_specs, check_vma=False
    )
```

```python
import functools

import jax
import jax.numpy as jnp
from jax import lax
from jax.experimental import pallas as pl
from jax.experimental.pallas import tpu as pltpu
from jax.sharding import PartitionSpec as P

HEAD_DIM = 128
NZ, NY, NC, NX = 8, 8, 2, 4
MESH = pl.DeviceIdType.MESH
F32, BF16, I32 = jnp.float32, jnp.bfloat16, jnp.int32
NN = (((1,), (0,)), ((), ()))
NT = (((1,), (1,)), ((), ()))
TN = (((0,), (0,)), ((), ()))


def dot(a, b, dims):
    return lax.dot_general(a, b, dims, preferred_element_type=F32)


def total(ref, slots):
    acc = ref[0].astype(F32)
    for i in range(1, slots):
        acc = acc + ref[i].astype(F32)
    return acc


def kernel(
    counts, source_h, offsets_h, mask_h, g_h, q_h, k_h, v_h, w_h,
    qg_out, kg_out, vg_out, wg_out,
    source, offsets, mask, q_v, w_v, g_all, g_other, gt,
    kv_own, rows, meta_own, meta, pick, sel, kv_in,
    att, att_other, back_own, back, spread, last,
    w_part, w_turn, w_turned, wz_send, wy_send, wz_in, wy_in, wz_go, wy_go, wz_pad, wy_pad, wz_last, wy_last,
    local_sem, pair_send, pair_recv, x_send, x_recv, send, recv, w_sent, w_recv,
):
    scale = HEAD_DIM ** -0.5
    dp, x = lax.axis_index("dp"), lax.axis_index("mp")
    z, y, c = lax.div(dp, NY * NC), lax.rem(lax.div(dp, NC), NY), lax.rem(dp, NC)
    slots, patches, cond, own = 4, 64, 16, 32
    width = q_v.shape[1]
    heads = width // HEAD_DIM

    def place(z, y, c):
        return ((z * NY + y) * NC + c, x)

    z_at = [lax.rem(z + k, NZ) for k in range(NZ)]
    y_at = [lax.rem(y + k, NY) for k in range(NY)]
    from_at = [jnp.where(c == 0, y_at[k], z_at[k]) for k in range(8)]
    to_at = [jnp.where(c == 0, z_at[k], y_at[k]) for k in range(8)]
    pair = place(z, y, 1 - c)
    x_peer = [((z * NY + y) * NC + c, lax.rem(x + k, NX)) for k in range(NX)]

    def on_z(k, core):
        return place(z_at[k], y, core)

    def on_y(k, core):
        return place(z, y_at[k], core)

    def on_from(k, core):
        return place(jnp.where(c == 0, z, z_at[k]), jnp.where(c == 0, y_at[k], y), core)

    def on_to(k, core):
        return place(jnp.where(c == 0, z_at[k], z), jnp.where(c == 0, y, y_at[k]), core)

    far_first = (4, 3, 5, 2, 6, 1, 7)
    started = []

    def push(src, dst, sent, got, device):
        copy = pltpu.make_async_remote_copy(
            src_ref=src, dst_ref=dst, send_sem=sent, recv_sem=got,
            device_id=device, device_id_type=MESH,
        )
        copy.start()
        started.append(copy)
        return copy

    def expect(dst, got):
        pltpu.make_async_remote_copy(
            src_ref=dst, dst_ref=dst, send_sem=pair_send.at[0], recv_sem=got,
            device_id=pair, device_id_type=MESH,
        ).wait_recv()

    def load(i, src, dst):
        copy = pltpu.make_async_copy(src, dst, local_sem.at[i])
        copy.start()
        return copy

    barrier = pltpu.get_barrier_semaphore()
    near = [pair] + x_peer[1:]
    for core in range(NC):
        near += [on_z(k, core) for k in range(1, NZ)] + [on_y(k, core) for k in range(1, NY)]
    for device in near:
        pl.semaphore_signal(barrier, inc=1, device_id=device, device_id_type=MESH)

    int_loads = [load(1, source_h, source), load(2, offsets_h, offsets)]
    load_k = load(3, k_h, kv_own.at[0])
    load_v = load(4, v_h, kv_own.at[1])
    load_g = load(5, g_h, g_all.at[x])
    load_m = load(6, mask_h, mask)
    load_q = load(7, q_h, q_v)
    load_w = load(8, w_h, w_v)

    for copy in int_loads:
        copy.wait()
    lane = lax.broadcasted_iota(I32, (8, 128), 1)
    slot, row = (lane >> 4) & 3, lane & 15
    named = jnp.full((8, 128), -(1 << 20), I32)
    for j in range(slots):
        first = jnp.where(j < counts[0], source[j] * own + offsets[j], -(1 << 20))
        named = jnp.where(slot == j, first + row, named)
    meta_own[...] = named
    meta[to_at[0], c] = named
    load_k.wait()
    load_v.wait()
    rows[from_at[0], c] = kv_own[c]
    load_g.wait()
    pl.semaphore_wait(barrier, len(near))

    for k in far_first:
        push(kv_own.at[0], rows.at[y, c], send.at[0, 0, k], recv.at[0, c, k], on_y(k, 0))
        push(kv_own.at[1], rows.at[z, c], send.at[0, 1, k], recv.at[0, c, k], on_z(k, 1))
    push(kv_own.at[1 - c], rows.at[to_at[0], c], send.at[0, 0, 0], recv.at[0, c, 0], pair)
    for k in far_first:
        push(meta_own, meta.at[z, c], send.at[1, 0, k], recv.at[1, c, k], on_z(k, 0))
        push(meta_own, meta.at[y, c], send.at[1, 1, k], recv.at[1, c, k], on_y(k, 1))
    push(meta_own, meta.at[from_at[0], c], send.at[1, 0, 0], recv.at[1, c, 0], pair)
    x_sent = [
        push(g_all.at[x], g_all.at[x], x_send.at[k], x_recv.at[k], x_peer[k]) for k in range(1, NX)
    ]
    g_pair = [push(g_all.at[x], g_other.at[x], pair_send.at[0], pair_recv.at[0], pair)]

    def arrive(line, dst):
        for k in range(1, 8):
            for core in range(NC):
                expect(dst, recv.at[line, core, k])
        expect(dst, recv.at[line, 1 - c, 0])

    def arrive_w(line, dst):
        for k in range(1, 8):
            expect(dst, w_recv.at[line, k])

    arrive(1, meta_own)
    left = lax.broadcasted_iota(I32, (1, 128), 1) < 64
    rows_of = lax.broadcasted_iota(I32, (512, 128), 0)
    for p in range(8):
        ids = jnp.where(left, meta[p, 0, 0:1, :], meta[p, 1, 0:1, :])
        ids_z, ids_y = ids >> 9, (ids >> 6) & 7
        keep = (ids >= 0) & (jnp.where(c == 0, ids_z, ids_y) == to_at[0])
        local = jnp.where(keep, jnp.where(c == 0, ids_y, ids_z) * 64 + (ids & 63), -1)
        pick[:, 128 * p : 128 * (p + 1)] = jnp.where(rows_of == local, 1.0, 0.0).astype(BF16)

    arrive(0, kv_own.at[0])
    sel[...] = (
        dot(pick[...], rows[...].reshape(512, width), TN).astype(BF16).reshape(8, 2, 64, width)
    )
    for k in far_first:
        for core in range(NC):
            push(
                sel.at[to_at[k], core], kv_in.at[c, to_at[0]],
                send.at[2, core, k], recv.at[2, c, k], on_to(k, core),
            )
    push(
        sel.at[to_at[0], 1 - c], kv_in.at[c, to_at[0]],
        send.at[2, 0, 0], recv.at[2, c, 0], pair,
    )
    kv_in[c, to_at[0]] = sel[to_at[0], c]

    for k in range(1, NX):
        x_sent[k - 1].wait_recv()
        came = lax.rem(x + NX - k, NX)
        g_pair.append(
            push(g_all.at[came], g_other.at[came], pair_send.at[k], pair_recv.at[k], pair)
        )
    load_w.wait()
    load_q.wait()
    load_m.wait()
    g = g_all[...].reshape(slots * patches, -1)
    ga = dot(g, w_v[...], NT).astype(BF16)
    gt[:, 0:256] = g.T
    for copy in g_pair:
        copy.wait_recv()
    gt[:, 256:512] = g_other[...].reshape(slots * patches, -1).T

    eye = lax.broadcasted_iota(I32, (cond, cond), 0) == lax.broadcasted_iota(I32, (cond, cond), 1)
    kept = jnp.concatenate(
        [
            jnp.sum(jnp.where(eye, mask[s : s + 1, :].astype(F32), 0.0), axis=1, keepdims=True)
            for s in range(slots)
        ],
        axis=0,
    )
    same_slot = (lax.broadcasted_iota(I32, (64, 256), 0) >> 4) == (
        lax.broadcasted_iota(I32, (64, 256), 1) >> 6
    )

    def grouped(a, op):
        a = a.reshape(slots, cond, 256)
        a = op(a, axis=1, keepdims=True)
        return jnp.broadcast_to(a, (slots, cond, 256)).reshape(64, 256)

    arrive(2, kv_in.at[0, 0])
    k_blocks = total(kv_in.at[0], 8).astype(BF16)
    v_blocks = total(kv_in.at[1], 8).astype(BF16)
    q = q_v[...]
    probs = []
    for h in range(heads):
        cols = slice(h * HEAD_DIM, (h + 1) * HEAD_DIM)
        scores = dot(k_blocks[:, cols], q[:, cols], NT) * scale
        scores = jnp.where(kept > 0.5, scores, -1e30)
        expos = jnp.exp(scores - grouped(scores, jnp.max))
        probs.append(jnp.where(same_slot, expos / grouped(expos, jnp.sum), 0.0))
        att[:, cols] = dot(probs[h].astype(BF16), v_blocks[:, cols], TN).astype(BF16)
    att_pair = push(att, att_other, pair_send.at[4], pair_recv.at[4], pair)

    dscores = []
    for h in range(heads):
        cols = slice(h * HEAD_DIM, (h + 1) * HEAD_DIM)
        probs_b = probs[h].astype(BF16)
        dprob = dot(v_blocks[:, cols], ga[:, cols], NT)
        delta = grouped(probs_b.astype(F32) * dprob, jnp.sum)
        dscore = (probs[h] * (dprob - delta)).astype(BF16)
        dscores.append(dscore)
        back_own[0, :, cols] = (dot(dscore, q[:, cols], NN) * scale).astype(BF16)
        back_own[1, :, cols] = dot(probs_b, ga[:, cols], NN).astype(BF16)
    for k in (1, 7):
        push(back_own.at[0], back.at[z, c], send.at[3, 0, k], recv.at[3, c, k], on_z(k, 0))
        push(back_own.at[1], back.at[y, c], send.at[3, 1, k], recv.at[3, c, k], on_y(k, 1))
    push(back_own.at[1 - c], back.at[from_at[0], c], send.at[3, 0, 0], recv.at[3, c, 0], pair)
    back[to_at[0], c] = back_own[c]

    def pass_on(far):
        for k, step in ((far, 1), (8 - far, 7)):
            if far == 3 and step == 7:
                continue
            for core in range(NC):
                expect(back_own.at[0], recv.at[3, core, k])
                block = back.at[to_at[8 - k], core]
                push(block, block, send.at[3, core, k + step - 8 * (step == 7)],
                     recv.at[3, core, k + step - 8 * (step == 7)], on_to(step, c))

    att_pair.wait_recv()
    for b in range(6):
        part = slice(b * 384, (b + 1) * 384)
        w_part[part, :] = (
            dot(gt[part, 0:256], att[...], NN) + dot(gt[part, 256:512], att_other[...], NN)
        ).astype(BF16)
    def parity(kept, first):
        i = lax.broadcasted_iota(I32, (8 * kept, 288), 0)
        a = sum((i >= kept * n).astype(I32) for n in range(1, 8))
        row = i + (36 - kept) * a + 18 * c + first
        return jnp.where(lax.broadcasted_iota(I32, (8 * kept, 288), 1) == row, 1.0, 0.0).astype(BF16)

    all_18, low_8, high_10 = parity(18, 0), parity(8, 0), parity(10, 8)
    for b in range(NZ):
        part = w_part[b * 288 : (b + 1) * 288, :]
        wz_send[b, 0:144, :] = dot(all_18, part[:, 0:128], NN).astype(BF16)
        wz_send[b, 144:208, :] = dot(low_8, part[:, 128:256], NN).astype(BF16)
        w_turn[b, 0:144, :] = dot(all_18, part[:, 256:384], NN)
        w_turn[b, 144:224, :] = dot(high_10, part[:, 128:256], NN)

    def first_hop(line, own_part, came, at, on):
        push(own_part.at[at[4]], came.at[1], w_sent.at[line, 1], w_recv.at[line, 1], on(1, c))
        push(own_part.at[at[5]], came.at[5], w_sent.at[line, 5], w_recv.at[line, 5], on(7, c))

    def next_hop(line, own_part, came, going, at, on, hop):
        for i, far, step in ((hop, 5 - hop, 1), (hop + 4, hop + 4, 7)):
            if i > 7:
                continue
            expect(came.at[0], w_recv.at[line, i - 1])
            going[i] = (came[i - 1].astype(F32) + own_part[at[far]].astype(F32)).astype(BF16)
            push(going.at[i], came.at[i], w_sent.at[line, i], w_recv.at[line, i], on(step, c))

    first_hop(0, wz_send, wz_in, z_at, on_z)
    pass_on(1)
    for b in range(NZ):
        for a in range(NY):
            w_turned[a, b * 18 : (b + 1) * 18, :] = w_turn[b, a * 18 : (a + 1) * 18, :]
            w_turned[a, 144 + b * 10 : 154 + b * 10, :] = w_turn[b, 144 + a * 10 : 154 + a * 10, :]
    wy_send[...] = w_turned[...].astype(BF16)
    first_hop(1, wy_send, wy_in, y_at, on_y)
    next_hop(0, wz_send, wz_in, wz_go, z_at, on_z, 2)
    next_hop(1, wy_send, wy_in, wy_go, y_at, on_y, 2)
    pass_on(2)
    next_hop(0, wz_send, wz_in, wz_go, z_at, on_z, 3)
    next_hop(1, wy_send, wy_in, wy_go, y_at, on_y, 3)
    pass_on(3)
    for h in range(heads):
        cols = slice(h * HEAD_DIM, (h + 1) * HEAD_DIM)
        qg_out[:, cols] = (dot(dscores[h], k_blocks[:, cols], TN) * scale).astype(BF16)

    next_hop(0, wz_send, wz_in, wz_go, z_at, on_z, 4)
    next_hop(1, wy_send, wy_in, wy_go, y_at, on_y, 4)
    for core in range(NC):
        for k in (4, 5):
            expect(back_own.at[0], recv.at[3, core, k])
    expect(back_own.at[0], recv.at[3, 1 - c, 0])
    spread[...] = (
        dot(pick[...], back[...].reshape(1024, width), NN).astype(BF16).reshape(8, 2, own, width)
    )
    for k in far_first:
        for core in range(NC):
            push(
                spread.at[from_at[k], core], last.at[c, from_at[0]],
                send.at[4, core, k], recv.at[4, c, k], on_from(k, core),
            )
    push(
        spread.at[from_at[0], 1 - c], last.at[c, from_at[0]],
        send.at[4, 0, 0], recv.at[4, c, 0], pair,
    )
    last[c, from_at[0]] = spread[from_at[0], c]

    def pad(tall, tail):
        o = lax.broadcasted_iota(I32, (256, tall), 0)
        a, i = o >> 5, o & 31
        row = jnp.where(i < 18, 18 * a + i, jnp.where(i < 18 + tail, 126 + tail * a + i, -1))
        return jnp.where(lax.broadcasted_iota(I32, (256, tall), 1) == row, 1.0, 0.0).astype(BF16)

    def summed(line, came, mine):
        expect(came.at[0], w_recv.at[line, 4])
        expect(came.at[0], w_recv.at[line, 7])
        return (came[4].astype(F32) + came[7].astype(F32) + mine.astype(F32)).astype(BF16)

    wy_pad[...] = dot(pad(224, 10), summed(1, wy_in, wy_send[y]), NN).astype(BF16).reshape(8, 32, 128)
    wy_last[z] = wy_pad[z]
    for k in far_first:
        push(wy_pad.at[z_at[k]], wy_last.at[z], w_sent.at[2, k], w_recv.at[2, k], on_z(k, c))
    wz_pad[...] = dot(pad(208, 8), summed(0, wz_in, wz_send[z]), NN).astype(BF16).reshape(8, 32, 128)
    wz_last[y] = wz_pad[y]
    for k in far_first:
        push(wz_pad.at[y_at[k]], wz_last.at[y], w_sent.at[3, k], w_recv.at[3, k], on_y(k, c))

    arrive(4, last.at[0, 0])
    kg_out[...] = total(last.at[0], 8).astype(BF16)
    vg_out[...] = total(last.at[1], 8).astype(BF16)
    arrive_w(2, wy_last.at[0])
    by_y = total(wy_last, NZ)
    wg_out[:, 256:384] = by_y[0:18, :]
    wg_out[8:18, 128:256] = by_y[18:28, :]
    arrive_w(3, wz_last.at[0])
    by_z = total(wz_last, NY)
    wg_out[:, 0:128] = by_z[0:18, :]
    wg_out[0:8, 128:256] = by_z[18:26, :]
    for copy in started:
        copy.wait_send()


def on_device(grad_out, queries, keys, values, out_weight, counts, source, offsets, key_mask):
    patches, d = grad_out.shape
    tokens, width = queries.shape
    own = keys.shape[0]
    slots, cond = key_mask.shape
    vmem = lambda *shape, dtype=BF16: pltpu.VMEM(shape, dtype)
    whole = pl.BlockSpec(memory_space=pltpu.VMEM)
    hbm = pl.BlockSpec(memory_space=pltpu.HBM)
    dma = lambda *shape: pltpu.SemaphoreType.DMA(shape)
    operands = (source, offsets, key_mask, grad_out, queries, keys, values, out_weight)
    operands = [pltpu.with_memory_space_constraint(a, pltpu.HBM) for a in operands]
    return pl.pallas_call(
        kernel,
        out_shape=(
            jax.ShapeDtypeStruct((tokens, width), BF16),
            jax.ShapeDtypeStruct((own, width), BF16),
            jax.ShapeDtypeStruct((own, width), BF16),
            jax.ShapeDtypeStruct((d // (NZ * NY * NC), width), F32),
        ),
        in_specs=[pl.BlockSpec(memory_space=pltpu.SMEM)] + [hbm] * 8,
        out_specs=(whole,) * 4,
        scratch_shapes=[
            pltpu.SMEM((slots,), I32), pltpu.SMEM((slots,), I32),
            vmem(slots, cond, dtype=I32),
            vmem(tokens, width), vmem(width, d), vmem(NX, patches, d), vmem(NX, patches, d),
            vmem(d, 512),
            vmem(2, own, width), vmem(8, NC, own, width),
            vmem(8, 128, dtype=I32), vmem(8, NC, 8, 128, dtype=I32),
            vmem(512, 1024), vmem(8, NC, 64, width), vmem(2, 8, 64, width),
            vmem(tokens, width), vmem(tokens, width),
            vmem(2, 64, width), vmem(8, NC, 64, width),
            vmem(8, NC, own, width), vmem(2, 8, own, width),
            vmem(d, width), vmem(NZ, 224, 128, dtype=F32), vmem(NY, 224, 128, dtype=F32),
            vmem(NZ, 208, 128), vmem(NY, 224, 128), vmem(NZ, 208, 128), vmem(NY, 224, 128),
            vmem(NZ, 208, 128), vmem(NY, 224, 128),
            vmem(NY, 32, 128), vmem(NZ, 32, 128), vmem(NY, 32, 128), vmem(NZ, 32, 128),
            dma(9), dma(5), dma(5), dma(NX), dma(NX),
            dma(5, 2, 8), dma(5, 2, 8), dma(4, 8), dma(4, 8),
        ],
        compiler_params=pltpu.CompilerParams(
            collective_id=0, has_side_effects=True, vmem_limit_bytes=48 << 20
        ),
        name="routed_attention_backward",
    )(counts, *operands)


def solution(mesh):
    in_specs = (
        P(("dp", "mp"), None),
        P("dp", "mp"),
        P("dp", "mp"),
        P("dp", "mp"),
        P("mp", None),
        P("dp"),
        P("dp"),
        P("dp"),
        P("dp", None),
    )
    out_specs = (P("dp", "mp"), P("dp", "mp"), P("dp", "mp"), P("dp", "mp"))
    return jax.shard_map(
        on_device, mesh=mesh, in_specs=in_specs, out_specs=out_specs, check_vma=False
    )
```

```python
import functools

import jax
import jax.numpy as jnp
from jax import lax
from jax.experimental import pallas as pl
from jax.experimental.pallas import tpu as pltpu
from jax.sharding import PartitionSpec as P

HEAD_DIM = 128
NZ, NY, NC, NX = 8, 8, 2, 4
MESH = pl.DeviceIdType.MESH
F32, BF16, I32 = jnp.float32, jnp.bfloat16, jnp.int32
NN = (((1,), (0,)), ((), ()))
NT = (((1,), (1,)), ((), ()))
TN = (((0,), (0,)), ((), ()))


def dot(a, b, dims):
    return lax.dot_general(a, b, dims, preferred_element_type=F32)


def total(ref, slots):
    acc = ref[0].astype(F32)
    for i in range(1, slots):
        acc = acc + ref[i].astype(F32)
    return acc


def kernel(
    counts, source_h, offsets_h, mask_h, g_h, q_h, k_h, v_h, w_h,
    out, wg_out,
    source, offsets, mask, q_v, w_v, g_all, g_other, gt,
    kv_own, rows, meta_own, meta, pick, sel, sel_came, sel_sum, kv_in,
    att, att_other, back_own, back, spread, last,
    w_part, w_turn, w_turned, wz_send, wy_send, wz_in, wy_in, wz_go, wy_go, wz_pad, wy_pad, wz_last, wy_last,
    local_sem, pair_send, pair_recv, x_send, x_recv, send, recv, w_sent, w_recv,
):
    scale = HEAD_DIM ** -0.5
    dp, x = lax.axis_index("dp"), lax.axis_index("mp")
    z, y, c = lax.div(dp, NY * NC), lax.rem(lax.div(dp, NC), NY), lax.rem(dp, NC)
    slots, patches, cond, own = 4, 64, 16, 32
    width = q_v.shape[1]
    heads = width // HEAD_DIM

    def place(z, y, c):
        return ((z * NY + y) * NC + c, x)

    z_at = [lax.rem(z + k, NZ) for k in range(NZ)]
    y_at = [lax.rem(y + k, NY) for k in range(NY)]
    from_at = [jnp.where(c == 0, y_at[k], z_at[k]) for k in range(8)]
    to_at = [jnp.where(c == 0, z_at[k], y_at[k]) for k in range(8)]
    pair = place(z, y, 1 - c)
    x_peer = [((z * NY + y) * NC + c, lax.rem(x + k, NX)) for k in range(NX)]

    def on_z(k, core):
        return place(z_at[k], y, core)

    def on_y(k, core):
        return place(z, y_at[k], core)

    def on_from(k, core):
        return place(jnp.where(c == 0, z, z_at[k]), jnp.where(c == 0, y_at[k], y), core)

    def on_to(k, core):
        return place(jnp.where(c == 0, z_at[k], z), jnp.where(c == 0, y, y_at[k]), core)

    far_first = (4, 3, 5, 2, 6, 1, 7)
    started = []

    def push(src, dst, sent, got, device):
        copy = pltpu.make_async_remote_copy(
            src_ref=src, dst_ref=dst, send_sem=sent, recv_sem=got,
            device_id=device, device_id_type=MESH,
        )
        copy.start()
        started.append(copy)
        return copy

    def expect(dst, got):
        pltpu.make_async_remote_copy(
            src_ref=dst, dst_ref=dst, send_sem=pair_send.at[0], recv_sem=got,
            device_id=pair, device_id_type=MESH,
        ).wait_recv()

    def load(i, src, dst):
        copy = pltpu.make_async_copy(src, dst, local_sem.at[i])
        copy.start()
        return copy

    barrier = pltpu.get_barrier_semaphore()
    near = [pair] + x_peer[1:]
    for core in range(NC):
        near += [on_z(k, core) for k in range(1, NZ)] + [on_y(k, core) for k in range(1, NY)]
    for device in near:
        pl.semaphore_signal(barrier, inc=1, device_id=device, device_id_type=MESH)

    int_loads = [load(1, source_h, source), load(2, offsets_h, offsets)]
    load_k = load(3, k_h, kv_own.at[0])
    load_v = load(4, v_h, kv_own.at[1])
    load_g = load(5, g_h, g_all.at[x])
    load_m = load(6, mask_h, mask)
    load_q = load(7, q_h, q_v)
    load_w = load(8, w_h, w_v)

    for copy in int_loads:
        copy.wait()
    lane = lax.broadcasted_iota(I32, (8, 128), 1)
    slot, row = (lane >> 4) & 3, lane & 15
    named = jnp.full((8, 128), -(1 << 20), I32)
    for j in range(slots):
        first = jnp.where(j < counts[0], source[j] * own + offsets[j], -(1 << 20))
        named = jnp.where(slot == j, first + row, named)
    meta_own[...] = named
    meta[to_at[0], c] = named
    load_k.wait()
    load_v.wait()
    rows[from_at[0], c] = kv_own[c]
    load_g.wait()
    pl.semaphore_wait(barrier, len(near))

    for k in far_first:
        push(kv_own.at[0], rows.at[y, c], send.at[0, 0, k], recv.at[0, c, k], on_y(k, 0))
        push(kv_own.at[1], rows.at[z, c], send.at[0, 1, k], recv.at[0, c, k], on_z(k, 1))
    push(kv_own.at[1 - c], rows.at[to_at[0], c], send.at[0, 0, 0], recv.at[0, c, 0], pair)
    for k in far_first:
        push(meta_own, meta.at[z, c], send.at[1, 0, k], recv.at[1, c, k], on_z(k, 0))
        push(meta_own, meta.at[y, c], send.at[1, 1, k], recv.at[1, c, k], on_y(k, 1))
    push(meta_own, meta.at[from_at[0], c], send.at[1, 0, 0], recv.at[1, c, 0], pair)
    x_sent = [
        push(g_all.at[x], g_all.at[x], x_send.at[k], x_recv.at[k], x_peer[k]) for k in range(1, NX)
    ]
    g_pair = [push(g_all.at[x], g_other.at[x], pair_send.at[0], pair_recv.at[0], pair)]

    def arrive(line, dst):
        for k in range(1, 8):
            for core in range(NC):
                expect(dst, recv.at[line, core, k])
        expect(dst, recv.at[line, 1 - c, 0])

    def arrive_w(line, dst):
        for k in range(1, 8):
            expect(dst, w_recv.at[line, k])

    arrive(1, meta_own)
    left = lax.broadcasted_iota(I32, (1, 128), 1) < 64
    rows_of = lax.broadcasted_iota(I32, (512, 128), 0)
    for p in range(8):
        ids = jnp.where(left, meta[p, 0, 0:1, :], meta[p, 1, 0:1, :])
        ids_z, ids_y = ids >> 9, (ids >> 6) & 7
        keep = (ids >= 0) & (jnp.where(c == 0, ids_z, ids_y) == to_at[0])
        local = jnp.where(keep, jnp.where(c == 0, ids_y, ids_z) * 64 + (ids & 63), -1)
        pick[:, 128 * p : 128 * (p + 1)] = jnp.where(rows_of == local, 1.0, 0.0).astype(BF16)

    arrive(0, kv_own.at[0])
    sel[...] = (
        dot(pick[...], rows[...].reshape(512, width), TN).astype(BF16).reshape(8, 2, 64, width)
    )
    steps = ((0, 1, 2, 3, 4), (1, 7, 6, 5, 8))
    parts = (pl.ds(0, 32), pl.ds(32, 32))
    for core in range(NC):
        for way, one, two, three, four in steps:
            push(sel.at[to_at[4], core, parts[way]], sel_came.at[way, 1, core, parts[way]],
                 send.at[2, core, four], recv.at[2, core, four], on_to(two, c))
            push(sel.at[to_at[three], core], sel_came.at[way, 0, core],
                 send.at[2, core, three], recv.at[2, core, three], on_to(one, c))
    for core in range(NC):
        for way, one, *_ in steps:
            push(sel.at[to_at[one], core], kv_in.at[c, 1 + way],
                 send.at[2, core, one], recv.at[2, c, one], on_to(one, core))
    push(sel.at[to_at[0], 1 - c], kv_in.at[c, 0], send.at[2, 0, 0], recv.at[2, c, 0], pair)
    kv_in[c, 0] = sel[to_at[0], c]
    for core in range(NC):
        for way, one, two, three, four in steps:
            expect(sel_came.at[0, 0, 0], recv.at[2, core, three])
            expect(sel_came.at[0, 0, 0, parts[0]], recv.at[2, core, four])
            part, rest = parts[way], parts[1 - way]
            sel_sum[way, core, part] = (
                sel[to_at[two], core, part] + sel_came[way, 0, core, part]
                + sel_came[way, 1, core, part]
            )
            sel_sum[way, core, rest] = sel[to_at[two], core, rest] + sel_came[way, 0, core, rest]
            push(sel_sum.at[way, core], kv_in.at[c, 3 + way],
                 send.at[2, core, two], recv.at[2, c, two], on_to(two, core))

    for k in range(1, NX):
        x_sent[k - 1].wait_recv()
        came = lax.rem(x + NX - k, NX)
        g_pair.append(
            push(g_all.at[came], g_other.at[came], pair_send.at[k], pair_recv.at[k], pair)
        )
    load_w.wait()
    load_q.wait()
    load_m.wait()
    g = g_all[...].reshape(slots * patches, -1)
    ga = dot(g, w_v[...], NT).astype(BF16)
    gt[:, 0:256] = g.T
    for copy in g_pair:
        copy.wait_recv()
    gt[:, 256:512] = g_other[...].reshape(slots * patches, -1).T

    eye = lax.broadcasted_iota(I32, (cond, cond), 0) == lax.broadcasted_iota(I32, (cond, cond), 1)
    kept = jnp.concatenate(
        [
            jnp.sum(jnp.where(eye, mask[s : s + 1, :].astype(F32), 0.0), axis=1, keepdims=True)
            for s in range(slots)
        ],
        axis=0,
    )
    same_slot = (lax.broadcasted_iota(I32, (64, 256), 0) >> 4) == (
        lax.broadcasted_iota(I32, (64, 256), 1) >> 6
    )

    def grouped(a, op):
        a = a.reshape(slots, cond, 256)
        a = op(a, axis=1, keepdims=True)
        return jnp.broadcast_to(a, (slots, cond, 256)).reshape(64, 256)

    for kind in range(2):
        for k in (1, 7, 2, 6):
            expect(kv_in.at[0, 0], recv.at[2, kind, k])
    expect(kv_in.at[0, 0], recv.at[2, 1 - c, 0])
    k_blocks = total(kv_in.at[0], 5).astype(BF16)
    v_blocks = total(kv_in.at[1], 5).astype(BF16)
    q = q_v[...]
    probs = []
    for h in range(heads):
        cols = slice(h * HEAD_DIM, (h + 1) * HEAD_DIM)
        scores = dot(k_blocks[:, cols], q[:, cols], NT) * scale
        scores = jnp.where(kept > 0.5, scores, -1e30)
        expos = jnp.exp(scores - grouped(scores, jnp.max))
        probs.append(jnp.where(same_slot, expos / grouped(expos, jnp.sum), 0.0))
        att[:, cols] = dot(probs[h].astype(BF16), v_blocks[:, cols], TN).astype(BF16)
    att_pair = push(att, att_other, pair_send.at[4], pair_recv.at[4], pair)

    dscores = []
    for h in range(heads):
        cols = slice(h * HEAD_DIM, (h + 1) * HEAD_DIM)
        probs_b = probs[h].astype(BF16)
        dprob = dot(v_blocks[:, cols], ga[:, cols], NT)
        delta = grouped(probs_b.astype(F32) * dprob, jnp.sum)
        dscore = (probs[h] * (dprob - delta)).astype(BF16)
        dscores.append(dscore)
        back_own[0, :, cols] = (dot(dscore, q[:, cols], NN) * scale).astype(BF16)
        back_own[1, :, cols] = dot(probs_b, ga[:, cols], NN).astype(BF16)
    for k in (2, 6, 1, 7):
        push(back_own.at[0], back.at[z, c], send.at[3, 0, k], recv.at[3, c, k], on_z(k, 0))
        push(back_own.at[1], back.at[y, c], send.at[3, 1, k], recv.at[3, c, k], on_y(k, 1))
    push(back_own.at[1 - c], back.at[from_at[0], c], send.at[3, 0, 0], recv.at[3, c, 0], pair)
    back[to_at[0], c] = back_own[c]

    def pass_on():
        for core in range(NC):
            for k, near, got, half, rest in ((2, 1, 3, 4, 0), (6, 7, 5, 8, 32)):
                expect(back_own.at[0], recv.at[3, core, k])
                block = back.at[to_at[8 - k], core]
                part = block.at[pl.ds(rest, 32)]
                push(block, block, send.at[3, core, got], recv.at[3, core, got], on_to(near, c))
                push(part, part, send.at[3, core, half], recv.at[3, core, half], on_to(k, c))

    att_pair.wait_recv()
    for b in range(6):
        part = slice(b * 384, (b + 1) * 384)
        w_part[part, :] = (
            dot(gt[part, 0:256], att[...], NN) + dot(gt[part, 256:512], att_other[...], NN)
        ).astype(BF16)
    def parity(kept, first):
        i = lax.broadcasted_iota(I32, (8 * kept, 288), 0)
        a = sum((i >= kept * n).astype(I32) for n in range(1, 8))
        row = i + (36 - kept) * a + 18 * c + first
        return jnp.where(lax.broadcasted_iota(I32, (8 * kept, 288), 1) == row, 1.0, 0.0).astype(BF16)

    all_18, low_8, high_10 = parity(18, 0), parity(8, 0), parity(10, 8)
    for b in range(NZ):
        part = w_part[b * 288 : (b + 1) * 288, :]
        wz_send[b, 0:144, :] = dot(all_18, part[:, 0:128], NN).astype(BF16)
        wz_send[b, 144:208, :] = dot(low_8, part[:, 128:256], NN).astype(BF16)
        w_turn[b, 0:144, :] = dot(all_18, part[:, 256:384], NN)
        w_turn[b, 144:224, :] = dot(high_10, part[:, 128:256], NN)

    def halves(tall):
        cut = tall // 32 * 16
        return (pl.ds(0, cut), pl.ds(cut, tall - cut))

    def first_hop(line, parts, came, at, on):
        for base, near, two, part in zip((0, 4), (1, 7), (2, 6), halves(parts.shape[1])):
            push(parts.at[at[4], part], came.at[base + 2, part],
                 w_sent.at[line, base + 2], w_recv.at[line, base + 2], on(two, c))
            push(parts.at[at[3 * near % 8]], came.at[base + 1],
                 w_sent.at[line, base + 1], w_recv.at[line, base + 1], on(near, c))
        for base, near in ((0, 1), (4, 7)):
            push(parts.at[at[near]], came.at[base],
                 w_sent.at[line, base], w_recv.at[line, base], on(near, c))

    def next_hop(line, parts, came, going, at, on):
        for base, two, part in zip((0, 4), (2, 6), halves(parts.shape[1])):
            expect(came.at[0], w_recv.at[line, base + 1])
            expect(came.at[0, part], w_recv.at[line, base + 2])
            going[base] = came[base + 1] + parts[at[two]]
            going[base, part] = (
                came[base + 1, part].astype(F32) + parts[at[two], part].astype(F32)
                + came[base + 2, part].astype(F32)
            ).astype(BF16)
            push(going.at[base], came.at[base + 3],
                 w_sent.at[line, base + 3], w_recv.at[line, base + 3], on(two, c))

    first_hop(0, wz_send, wz_in, z_at, on_z)
    for b in range(NZ):
        for a in range(NY):
            w_turned[a, b * 18 : (b + 1) * 18, :] = w_turn[b, a * 18 : (a + 1) * 18, :]
            w_turned[a, 144 + b * 10 : 154 + b * 10, :] = w_turn[b, 144 + a * 10 : 154 + a * 10, :]
    wy_send[...] = w_turned[...].astype(BF16)
    first_hop(1, wy_send, wy_in, y_at, on_y)
    pass_on()
    next_hop(0, wz_send, wz_in, wz_go, z_at, on_z)
    next_hop(1, wy_send, wy_in, wy_go, y_at, on_y)
    for h in range(heads):
        cols = slice(h * HEAD_DIM, (h + 1) * HEAD_DIM)
        out[0:256, cols] = (dot(dscores[h], k_blocks[:, cols], TN) * scale).astype(BF16)

    for core in range(NC):
        for k in (1, 7, 3, 5):
            expect(back_own.at[0], recv.at[3, core, k])
        for k in (4, 8):
            expect(back_own.at[0, pl.ds(0, 32)], recv.at[3, core, k])
    expect(back_own.at[0], recv.at[3, 1 - c, 0])
    spread[...] = (
        dot(pick[...], back[...].reshape(1024, width), NN).astype(BF16).reshape(8, 2, own, width)
    )
    for k in far_first:
        for core in range(NC):
            push(
                spread.at[from_at[k], core], last.at[c, from_at[0]],
                send.at[4, core, k], recv.at[4, c, k], on_from(k, core),
            )
    push(
        spread.at[from_at[0], 1 - c], last.at[c, from_at[0]],
        send.at[4, 0, 0], recv.at[4, c, 0], pair,
    )
    last[c, from_at[0]] = spread[from_at[0], c]

    def pad(tall, tail):
        o = lax.broadcasted_iota(I32, (256, tall), 0)
        a, i = o >> 5, o & 31
        row = jnp.where(i < 18, 18 * a + i, jnp.where(i < 18 + tail, 126 + tail * a + i, -1))
        return jnp.where(lax.broadcasted_iota(I32, (256, tall), 1) == row, 1.0, 0.0).astype(BF16)

    def summed(line, came, mine):
        for i in (0, 3, 4, 7):
            expect(came.at[0], w_recv.at[line, i])
            mine = mine.astype(F32) + came[i].astype(F32)
        return mine.astype(BF16)


    wy_pad[...] = dot(pad(224, 10), summed(1, wy_in, wy_send[y]), NN).astype(BF16).reshape(8, 32, 128)
    wy_last[z] = wy_pad[z]
    for k in far_first:
        push(wy_pad.at[z_at[k]], wy_last.at[z], w_sent.at[2, k], w_recv.at[2, k], on_z(k, c))
    wz_pad[...] = dot(pad(208, 8), summed(0, wz_in, wz_send[z]), NN).astype(BF16).reshape(8, 32, 128)
    wz_last[y] = wz_pad[y]
    for k in far_first:
        push(wz_pad.at[y_at[k]], wz_last.at[y], w_sent.at[3, k], w_recv.at[3, k], on_y(k, c))

    arrive(4, last.at[0, 0])
    out[256:288, :] = total(last.at[0], 8).astype(BF16)
    out[288:320, :] = total(last.at[1], 8).astype(BF16)
    arrive_w(2, wy_last.at[0])
    by_y = total(wy_last, NZ)
    wg_out[:, 256:384] = by_y[0:18, :]
    wg_out[8:18, 128:256] = by_y[18:28, :]
    arrive_w(3, wz_last.at[0])
    by_z = total(wz_last, NY)
    wg_out[:, 0:128] = by_z[0:18, :]
    wg_out[0:8, 128:256] = by_z[18:26, :]
    for copy in started:
        copy.wait_send()


def on_device(grad_out, queries, keys, values, out_weight, counts, source, offsets, key_mask):
    patches, d = grad_out.shape
    tokens, width = queries.shape
    own = keys.shape[0]
    slots, cond = key_mask.shape
    vmem = lambda *shape, dtype=BF16: pltpu.VMEM(shape, dtype)
    whole = pl.BlockSpec(memory_space=pltpu.VMEM)
    hbm = pl.BlockSpec(memory_space=pltpu.HBM)
    dma = lambda *shape: pltpu.SemaphoreType.DMA(shape)
    operands = (source, offsets, key_mask, grad_out, queries, keys, values, out_weight)
    operands = [pltpu.with_memory_space_constraint(a, pltpu.HBM) for a in operands]
    packed, wg = pl.pallas_call(
        kernel,
        out_shape=(
            jax.ShapeDtypeStruct((tokens + 2 * own, width), BF16),
            jax.ShapeDtypeStruct((d // (NZ * NY * NC), width), F32),
        ),
        in_specs=[pl.BlockSpec(memory_space=pltpu.SMEM)] + [hbm] * 8,
        out_specs=(whole,) * 2,
        scratch_shapes=[
            pltpu.SMEM((slots,), I32), pltpu.SMEM((slots,), I32),
            vmem(slots, cond, dtype=I32),
            vmem(tokens, width), vmem(width, d), vmem(NX, patches, d), vmem(NX, patches, d),
            vmem(d, 512),
            vmem(2, own, width), vmem(8, NC, own, width),
            vmem(8, 128, dtype=I32), vmem(8, NC, 8, 128, dtype=I32),
            vmem(512, 1024), vmem(8, NC, 64, width),
            vmem(2, 2, NC, 64, width), vmem(2, NC, 64, width), vmem(2, 5, 64, width),
            vmem(tokens, width), vmem(tokens, width),
            vmem(2, 64, width), vmem(8, NC, 64, width),
            vmem(8, NC, own, width), vmem(2, 8, own, width),
            vmem(d, width), vmem(NZ, 224, 128, dtype=F32), vmem(NY, 224, 128, dtype=F32),
            vmem(NZ, 208, 128), vmem(NY, 224, 128), vmem(NZ, 208, 128), vmem(NY, 224, 128),
            vmem(NZ, 208, 128), vmem(NY, 224, 128),
            vmem(NY, 32, 128), vmem(NZ, 32, 128), vmem(NY, 32, 128), vmem(NZ, 32, 128),
            dma(9), dma(5), dma(5), dma(NX), dma(NX),
            dma(5, 2, 9), dma(5, 2, 9), dma(4, 8), dma(4, 8),
        ],
        compiler_params=pltpu.CompilerParams(
            collective_id=0, has_side_effects=True, vmem_limit_bytes=48 << 20
        ),
        name="routed_attention_backward",
    )(counts, *operands)
    return packed[:tokens], packed[tokens : tokens + own], packed[tokens + own :], wg


def solution(mesh):
    in_specs = (
        P(("dp", "mp"), None),
        P("dp", "mp"),
        P("dp", "mp"),
        P("dp", "mp"),
        P("mp", None),
        P("dp"),
        P("dp"),
        P("dp"),
        P("dp", None),
    )
    out_specs = (P("dp", "mp"), P("dp", "mp"), P("dp", "mp"), P("dp", "mp"))
    return jax.shard_map(
        on_device, mesh=mesh, in_specs=in_specs, out_specs=out_specs, check_vma=False
    )
```

```python
import functools

import jax
import jax.numpy as jnp
from jax import lax
from jax.experimental import pallas as pl
from jax.experimental.pallas import tpu as pltpu
from jax.sharding import PartitionSpec as P

HEAD_DIM = 128
NZ, NY, NC, NX = 8, 8, 2, 4
MESH = pl.DeviceIdType.MESH
F32, BF16, I32 = jnp.float32, jnp.bfloat16, jnp.int32
NN = (((1,), (0,)), ((), ()))
NT = (((1,), (1,)), ((), ()))
TN = (((0,), (0,)), ((), ()))


def dot(a, b, dims):
    return lax.dot_general(a, b, dims, preferred_element_type=F32)


def total(ref, slots):
    acc = ref[0].astype(F32)
    for i in range(1, slots):
        acc = acc + ref[i].astype(F32)
    return acc


def kernel(
    counts, source_h, offsets_h, mask_h, g_h, q_h, k_h, v_h, w_h,
    out, wg_out,
    source, offsets, mask, q_v, w_v, g_all, g_other, gt,
    kv_own, rows, meta_own, meta, pick, sel, sel_came, sel_sum, kv_in,
    att, att_other, back_own, back, spread, last_came, last_sum, last,
    w_part, w_turn, w_turned, wz_send, wy_send, wz_in, wy_in, wz_go, wy_go, wz_pad, wy_pad, wz_last, wy_last,
    local_sem, pair_send, pair_recv, x_send, x_recv, send, recv, w_sent, w_recv,
):
    scale = HEAD_DIM ** -0.5
    dp, x = lax.axis_index("dp"), lax.axis_index("mp")
    z, y, c = lax.div(dp, NY * NC), lax.rem(lax.div(dp, NC), NY), lax.rem(dp, NC)
    slots, patches, cond, own = 4, 64, 16, 32
    width = q_v.shape[1]
    heads = width // HEAD_DIM

    def place(z, y, c):
        return ((z * NY + y) * NC + c, x)

    z_at = [lax.rem(z + k, NZ) for k in range(NZ)]
    y_at = [lax.rem(y + k, NY) for k in range(NY)]
    from_at = [jnp.where(c == 0, y_at[k], z_at[k]) for k in range(8)]
    to_at = [jnp.where(c == 0, z_at[k], y_at[k]) for k in range(8)]
    pair = place(z, y, 1 - c)
    x_peer = [((z * NY + y) * NC + c, lax.rem(x + k, NX)) for k in range(NX)]

    def on_z(k, core):
        return place(z_at[k], y, core)

    def on_y(k, core):
        return place(z, y_at[k], core)

    def on_from(k, core):
        return place(jnp.where(c == 0, z, z_at[k]), jnp.where(c == 0, y_at[k], y), core)

    def on_to(k, core):
        return place(jnp.where(c == 0, z_at[k], z), jnp.where(c == 0, y, y_at[k]), core)

    far_first = (4, 3, 5, 2, 6, 1, 7)
    started = []

    def push(src, dst, sent, got, device):
        copy = pltpu.make_async_remote_copy(
            src_ref=src, dst_ref=dst, send_sem=sent, recv_sem=got,
            device_id=device, device_id_type=MESH,
        )
        copy.start()
        started.append(copy)
        return copy

    def expect(dst, got):
        pltpu.make_async_remote_copy(
            src_ref=dst, dst_ref=dst, send_sem=pair_send.at[0], recv_sem=got,
            device_id=pair, device_id_type=MESH,
        ).wait_recv()

    def load(i, src, dst):
        copy = pltpu.make_async_copy(src, dst, local_sem.at[i])
        copy.start()
        return copy

    barrier = pltpu.get_barrier_semaphore()
    near = [pair] + x_peer[1:]
    for core in range(NC):
        near += [on_z(k, core) for k in range(1, NZ)] + [on_y(k, core) for k in range(1, NY)]
    for device in near:
        pl.semaphore_signal(barrier, inc=1, device_id=device, device_id_type=MESH)

    int_loads = [load(1, source_h, source), load(2, offsets_h, offsets)]
    load_k = load(3, k_h, kv_own.at[0])
    load_v = load(4, v_h, kv_own.at[1])
    load_g = load(5, g_h, g_all.at[x])
    load_m = load(6, mask_h, mask)
    load_q = load(7, q_h, q_v)
    load_w = load(8, w_h, w_v)

    for copy in int_loads:
        copy.wait()
    lane = lax.broadcasted_iota(I32, (8, 128), 1)
    slot, row = (lane >> 4) & 3, lane & 15
    named = jnp.full((8, 128), -(1 << 20), I32)
    for j in range(slots):
        first = jnp.where(j < counts[0], source[j] * own + offsets[j], -(1 << 20))
        named = jnp.where(slot == j, first + row, named)
    meta_own[...] = named
    meta[to_at[0], c] = named
    load_k.wait()
    load_v.wait()
    rows[from_at[0], c] = kv_own[c]
    load_g.wait()
    pl.semaphore_wait(barrier, len(near))

    for k in far_first:
        push(meta_own, meta.at[z, c], send.at[1, 0, k], recv.at[1, c, k], on_z(k, 0))
        push(meta_own, meta.at[y, c], send.at[1, 1, k], recv.at[1, c, k], on_y(k, 1))
    push(meta_own, meta.at[from_at[0], c], send.at[1, 0, 0], recv.at[1, c, 0], pair)
    for k in far_first:
        push(kv_own.at[0], rows.at[y, c], send.at[0, 0, k], recv.at[0, c, k], on_y(k, 0))
        push(kv_own.at[1], rows.at[z, c], send.at[0, 1, k], recv.at[0, c, k], on_z(k, 1))
    push(kv_own.at[1 - c], rows.at[to_at[0], c], send.at[0, 0, 0], recv.at[0, c, 0], pair)
    x_sent = [
        push(g_all.at[x], g_all.at[x], x_send.at[k], x_recv.at[k], x_peer[k]) for k in range(1, NX)
    ]
    g_pair = [push(g_all.at[x], g_other.at[x], pair_send.at[0], pair_recv.at[0], pair)]

    def arrive(line, dst):
        for k in range(1, 8):
            for core in range(NC):
                expect(dst, recv.at[line, core, k])
        expect(dst, recv.at[line, 1 - c, 0])

    def arrive_w(line, dst):
        for k in range(1, 8):
            expect(dst, w_recv.at[line, k])

    arrive(1, meta_own)
    left = lax.broadcasted_iota(I32, (1, 128), 1) < 64
    rows_of = lax.broadcasted_iota(I32, (512, 128), 0)
    for p in range(8):
        ids = jnp.where(left, meta[p, 0, 0:1, :], meta[p, 1, 0:1, :])
        ids_z, ids_y = ids >> 9, (ids >> 6) & 7
        keep = (ids >= 0) & (jnp.where(c == 0, ids_z, ids_y) == to_at[0])
        local = jnp.where(keep, jnp.where(c == 0, ids_y, ids_z) * 64 + (ids & 63), -1)
        pick[:, 128 * p : 128 * (p + 1)] = jnp.where(rows_of == local, 1.0, 0.0).astype(BF16)

    arrive(0, kv_own.at[0])
    sel[...] = (
        dot(pick[...], rows[...].reshape(512, width), TN).astype(BF16).reshape(8, 2, 64, width)
    )
    steps = ((0, 1, 2, 3, 4), (1, 7, 6, 5, 8))
    parts = (pl.ds(0, 32), pl.ds(32, 32))
    for core in range(NC):
        for way, one, two, three, four in steps:
            push(sel.at[to_at[4], core, parts[way]], sel_came.at[way, 1, core, parts[way]],
                 send.at[2, core, four], recv.at[2, core, four], on_to(two, c))
            push(sel.at[to_at[three], core], sel_came.at[way, 0, core],
                 send.at[2, core, three], recv.at[2, core, three], on_to(one, c))
    for core in range(NC):
        for way, one, *_ in steps:
            push(sel.at[to_at[one], core], kv_in.at[c, 1 + way],
                 send.at[2, core, one], recv.at[2, c, one], on_to(one, core))
    push(sel.at[to_at[0], 1 - c], kv_in.at[c, 0], send.at[2, 0, 0], recv.at[2, c, 0], pair)
    kv_in[c, 0] = sel[to_at[0], c]
    for core in range(NC):
        for way, one, two, three, four in steps:
            expect(sel_came.at[0, 0, 0], recv.at[2, core, three])
            expect(sel_came.at[0, 0, 0, parts[0]], recv.at[2, core, four])
            part, rest = parts[way], parts[1 - way]
            sel_sum[way, core, part] = (
                sel[to_at[two], core, part] + sel_came[way, 0, core, part]
                + sel_came[way, 1, core, part]
            )
            sel_sum[way, core, rest] = sel[to_at[two], core, rest] + sel_came[way, 0, core, rest]
            push(sel_sum.at[way, core], kv_in.at[c, 3 + way],
                 send.at[2, core, two], recv.at[2, c, two], on_to(two, core))

    for k in range(1, NX):
        x_sent[k - 1].wait_recv()
        came = lax.rem(x + NX - k, NX)
        g_pair.append(
            push(g_all.at[came], g_other.at[came], pair_send.at[k], pair_recv.at[k], pair)
        )
    load_w.wait()
    load_q.wait()
    load_m.wait()
    g = g_all[...].reshape(slots * patches, -1)
    ga = dot(g, w_v[...], NT).astype(BF16)
    gt[:, 0:256] = g.T
    for copy in g_pair:
        copy.wait_recv()
    gt[:, 256:512] = g_other[...].reshape(slots * patches, -1).T

    eye = lax.broadcasted_iota(I32, (cond, cond), 0) == lax.broadcasted_iota(I32, (cond, cond), 1)
    kept = jnp.concatenate(
        [
            jnp.sum(jnp.where(eye, mask[s : s + 1, :].astype(F32), 0.0), axis=1, keepdims=True)
            for s in range(slots)
        ],
        axis=0,
    )
    same_slot = (lax.broadcasted_iota(I32, (64, 256), 0) >> 4) == (
        lax.broadcasted_iota(I32, (64, 256), 1) >> 6
    )

    def grouped(a, op):
        a = a.reshape(slots, cond, 256)
        a = op(a, axis=1, keepdims=True)
        return jnp.broadcast_to(a, (slots, cond, 256)).reshape(64, 256)

    for kind in range(2):
        for k in (1, 7, 2, 6):
            expect(kv_in.at[0, 0], recv.at[2, kind, k])
    expect(kv_in.at[0, 0], recv.at[2, 1 - c, 0])
    k_blocks = total(kv_in.at[0], 5).astype(BF16)
    v_blocks = total(kv_in.at[1], 5).astype(BF16)
    q = q_v[...]
    probs = []
    for h in range(heads):
        cols = slice(h * HEAD_DIM, (h + 1) * HEAD_DIM)
        scores = dot(k_blocks[:, cols], q[:, cols], NT) * scale
        scores = jnp.where(kept > 0.5, scores, -1e30)
        expos = jnp.exp(scores - grouped(scores, jnp.max))
        probs.append(jnp.where(same_slot, expos / grouped(expos, jnp.sum), 0.0))
        att[:, cols] = dot(probs[h].astype(BF16), v_blocks[:, cols], TN).astype(BF16)
    att_pair = push(att, att_other, pair_send.at[4], pair_recv.at[4], pair)

    dscores = []
    for h in range(heads):
        cols = slice(h * HEAD_DIM, (h + 1) * HEAD_DIM)
        probs_b = probs[h].astype(BF16)
        dprob = dot(v_blocks[:, cols], ga[:, cols], NT)
        delta = grouped(probs_b.astype(F32) * dprob, jnp.sum)
        dscore = (probs[h] * (dprob - delta)).astype(BF16)
        dscores.append(dscore)
        back_own[0, :, cols] = (dot(dscore, q[:, cols], NN) * scale).astype(BF16)
        back_own[1, :, cols] = dot(probs_b, ga[:, cols], NN).astype(BF16)
    for k in (2, 6, 1, 7):
        push(back_own.at[0], back.at[z, c], send.at[3, 0, k], recv.at[3, c, k], on_z(k, 0))
        push(back_own.at[1], back.at[y, c], send.at[3, 1, k], recv.at[3, c, k], on_y(k, 1))
    push(back_own.at[1 - c], back.at[from_at[0], c], send.at[3, 0, 0], recv.at[3, c, 0], pair)
    back[to_at[0], c] = back_own[c]

    def pass_on():
        for core in range(NC):
            for k, near, got, half, rest in ((2, 1, 3, 4, 0), (6, 7, 5, 8, 32)):
                expect(back_own.at[0], recv.at[3, core, k])
                block = back.at[to_at[8 - k], core]
                part = block.at[pl.ds(rest, 32)]
                push(block, block, send.at[3, core, got], recv.at[3, core, got], on_to(near, c))
                push(part, part, send.at[3, core, half], recv.at[3, core, half], on_to(k, c))

    att_pair.wait_recv()
    for b in range(6):
        part = slice(b * 384, (b + 1) * 384)
        w_part[part, :] = (
            dot(gt[part, 0:256], att[...], NN) + dot(gt[part, 256:512], att_other[...], NN)
        ).astype(BF16)
    def parity(kept, first):
        i = lax.broadcasted_iota(I32, (8 * kept, 288), 0)
        a = sum((i >= kept * n).astype(I32) for n in range(1, 8))
        row = i + (36 - kept) * a + 18 * c + first
        return jnp.where(lax.broadcasted_iota(I32, (8 * kept, 288), 1) == row, 1.0, 0.0).astype(BF16)

    all_18, low_8, high_10 = parity(18, 0), parity(8, 0), parity(10, 8)
    for b in range(NZ):
        part = w_part[b * 288 : (b + 1) * 288, :]
        wz_send[b, 0:144, :] = dot(all_18, part[:, 0:128], NN).astype(BF16)
        wz_send[b, 144:208, :] = dot(low_8, part[:, 128:256], NN).astype(BF16)
        w_turn[b, 0:144, :] = dot(all_18, part[:, 256:384], NN)
        w_turn[b, 144:224, :] = dot(high_10, part[:, 128:256], NN)

    def halves(tall):
        cut = tall // 32 * 16
        return (pl.ds(0, cut), pl.ds(cut, tall - cut))

    def first_hop(line, parts, came, at, on):
        for base, near, two, part in zip((0, 4), (1, 7), (2, 6), halves(parts.shape[1])):
            push(parts.at[at[4], part], came.at[base + 2, part],
                 w_sent.at[line, base + 2], w_recv.at[line, base + 2], on(two, c))
            push(parts.at[at[3 * near % 8]], came.at[base + 1],
                 w_sent.at[line, base + 1], w_recv.at[line, base + 1], on(near, c))
        for base, near in ((0, 1), (4, 7)):
            push(parts.at[at[near]], came.at[base],
                 w_sent.at[line, base], w_recv.at[line, base], on(near, c))

    def next_hop(line, parts, came, going, at, on):
        for base, two, part in zip((0, 4), (2, 6), halves(parts.shape[1])):
            expect(came.at[0], w_recv.at[line, base + 1])
            expect(came.at[0, part], w_recv.at[line, base + 2])
            going[base] = came[base + 1] + parts[at[two]]
            going[base, part] = (
                came[base + 1, part].astype(F32) + parts[at[two], part].astype(F32)
                + came[base + 2, part].astype(F32)
            ).astype(BF16)
            push(going.at[base], came.at[base + 3],
                 w_sent.at[line, base + 3], w_recv.at[line, base + 3], on(two, c))

    first_hop(0, wz_send, wz_in, z_at, on_z)
    for b in range(NZ):
        for a in range(NY):
            w_turned[a, b * 18 : (b + 1) * 18, :] = w_turn[b, a * 18 : (a + 1) * 18, :]
            w_turned[a, 144 + b * 10 : 154 + b * 10, :] = w_turn[b, 144 + a * 10 : 154 + a * 10, :]
    wy_send[...] = w_turned[...].astype(BF16)
    first_hop(1, wy_send, wy_in, y_at, on_y)
    pass_on()
    next_hop(0, wz_send, wz_in, wz_go, z_at, on_z)
    next_hop(1, wy_send, wy_in, wy_go, y_at, on_y)
    for h in range(heads):
        cols = slice(h * HEAD_DIM, (h + 1) * HEAD_DIM)
        out[0:256, cols] = (dot(dscores[h], k_blocks[:, cols], TN) * scale).astype(BF16)

    for core in range(NC):
        for k in (1, 7, 3, 5):
            expect(back_own.at[0], recv.at[3, core, k])
        for k in (4, 8):
            expect(back_own.at[0, pl.ds(0, 32)], recv.at[3, core, k])
    expect(back_own.at[0], recv.at[3, 1 - c, 0])
    spread[...] = (
        dot(pick[...], back[...].reshape(1024, width), NN).astype(BF16).reshape(8, 2, own, width)
    )
    parts = (pl.ds(0, 16), pl.ds(16, 16))
    for core in range(NC):
        for way, one, two, three, four in steps:
            push(spread.at[from_at[4], core, parts[way]], last_came.at[way, 1, core, parts[way]],
                 send.at[4, core, four], recv.at[4, core, four], on_from(two, c))
            push(spread.at[from_at[three], core], last_came.at[way, 0, core],
                 send.at[4, core, three], recv.at[4, core, three], on_from(one, c))
    for core in range(NC):
        for way, one, *_ in steps:
            push(spread.at[from_at[one], core], last.at[c, 1 + way],
                 send.at[4, core, one], recv.at[4, c, one], on_from(one, core))
    push(spread.at[from_at[0], 1 - c], last.at[c, 0], send.at[4, 0, 0], recv.at[4, c, 0], pair)
    last[c, 0] = spread[from_at[0], c]

    def pad(tall, tail):
        o = lax.broadcasted_iota(I32, (256, tall), 0)
        a, i = o >> 5, o & 31
        row = jnp.where(i < 18, 18 * a + i, jnp.where(i < 18 + tail, 126 + tail * a + i, -1))
        return jnp.where(lax.broadcasted_iota(I32, (256, tall), 1) == row, 1.0, 0.0).astype(BF16)

    def summed(line, came, mine):
        for i in (0, 3, 4, 7):
            expect(came.at[0], w_recv.at[line, i])
            mine = mine.astype(F32) + came[i].astype(F32)
        return mine.astype(BF16)


    wy_pad[...] = dot(pad(224, 10), summed(1, wy_in, wy_send[y]), NN).astype(BF16).reshape(8, 32, 128)
    wy_last[z] = wy_pad[z]
    for k in far_first:
        push(wy_pad.at[z_at[k]], wy_last.at[z], w_sent.at[2, k], w_recv.at[2, k], on_z(k, c))
    wz_pad[...] = dot(pad(208, 8), summed(0, wz_in, wz_send[z]), NN).astype(BF16).reshape(8, 32, 128)
    wz_last[y] = wz_pad[y]
    for k in far_first:
        push(wz_pad.at[y_at[k]], wz_last.at[y], w_sent.at[3, k], w_recv.at[3, k], on_y(k, c))

    for core in range(NC):
        for way, one, two, three, four in steps:
            expect(last_came.at[0, 0, 0], recv.at[4, core, three])
            expect(last_came.at[0, 0, 0, parts[0]], recv.at[4, core, four])
            part, rest = parts[way], parts[1 - way]
            last_sum[way, core, part] = (
                spread[from_at[two], core, part] + last_came[way, 0, core, part]
                + last_came[way, 1, core, part]
            )
            last_sum[way, core, rest] = spread[from_at[two], core, rest] + last_came[way, 0, core, rest]
            push(last_sum.at[way, core], last.at[c, 3 + way],
                 send.at[4, core, two], recv.at[4, c, two], on_from(two, core))
    for kind in range(2):
        for k in (1, 7, 2, 6):
            expect(last.at[0, 0], recv.at[4, kind, k])
    expect(last.at[0, 0], recv.at[4, 1 - c, 0])
    out[256:288, :] = total(last.at[0], 5).astype(BF16)
    out[288:320, :] = total(last.at[1], 5).astype(BF16)
    arrive_w(2, wy_last.at[0])
    by_y = total(wy_last, NZ)
    wg_out[:, 256:384] = by_y[0:18, :]
    wg_out[8:18, 128:256] = by_y[18:28, :]
    arrive_w(3, wz_last.at[0])
    by_z = total(wz_last, NY)
    wg_out[:, 0:128] = by_z[0:18, :]
    wg_out[0:8, 128:256] = by_z[18:26, :]
    for copy in started:
        copy.wait_send()


def on_device(grad_out, queries, keys, values, out_weight, counts, source, offsets, key_mask):
    patches, d = grad_out.shape
    tokens, width = queries.shape
    own = keys.shape[0]
    slots, cond = key_mask.shape
    vmem = lambda *shape, dtype=BF16: pltpu.VMEM(shape, dtype)
    whole = pl.BlockSpec(memory_space=pltpu.VMEM)
    hbm = pl.BlockSpec(memory_space=pltpu.HBM)
    dma = lambda *shape: pltpu.SemaphoreType.DMA(shape)
    operands = (source, offsets, key_mask, grad_out, queries, keys, values, out_weight)
    operands = [pltpu.with_memory_space_constraint(a, pltpu.HBM) for a in operands]
    packed, wg = pl.pallas_call(
        kernel,
        out_shape=(
            jax.ShapeDtypeStruct((tokens + 2 * own, width), BF16),
            jax.ShapeDtypeStruct((d // (NZ * NY * NC), width), F32),
        ),
        in_specs=[pl.BlockSpec(memory_space=pltpu.SMEM)] + [hbm] * 8,
        out_specs=(whole,) * 2,
        scratch_shapes=[
            pltpu.SMEM((slots,), I32), pltpu.SMEM((slots,), I32),
            vmem(slots, cond, dtype=I32),
            vmem(tokens, width), vmem(width, d), vmem(NX, patches, d), vmem(NX, patches, d),
            vmem(d, 512),
            vmem(2, own, width), vmem(8, NC, own, width),
            vmem(8, 128, dtype=I32), vmem(8, NC, 8, 128, dtype=I32),
            vmem(512, 1024), vmem(8, NC, 64, width),
            vmem(2, 2, NC, 64, width), vmem(2, NC, 64, width), vmem(2, 5, 64, width),
            vmem(tokens, width), vmem(tokens, width),
            vmem(2, 64, width), vmem(8, NC, 64, width),
            vmem(8, NC, own, width),
            vmem(2, 2, NC, own, width), vmem(2, NC, own, width), vmem(2, 5, own, width),
            vmem(d, width), vmem(NZ, 224, 128, dtype=F32), vmem(NY, 224, 128, dtype=F32),
            vmem(NZ, 208, 128), vmem(NY, 224, 128), vmem(NZ, 208, 128), vmem(NY, 224, 128),
            vmem(NZ, 208, 128), vmem(NY, 224, 128),
            vmem(NY, 32, 128), vmem(NZ, 32, 128), vmem(NY, 32, 128), vmem(NZ, 32, 128),
            dma(9), dma(5), dma(5), dma(NX), dma(NX),
            dma(5, 2, 9), dma(5, 2, 9), dma(4, 8), dma(4, 8),
        ],
        compiler_params=pltpu.CompilerParams(
            collective_id=0, has_side_effects=True, vmem_limit_bytes=48 << 20
        ),
        name="routed_attention_backward",
    )(counts, *operands)
    return packed[:tokens], packed[tokens : tokens + own], packed[tokens + own :], wg


def solution(mesh):
    in_specs = (
        P(("dp", "mp"), None),
        P("dp", "mp"),
        P("dp", "mp"),
        P("dp", "mp"),
        P("mp", None),
        P("dp"),
        P("dp"),
        P("dp"),
        P("dp", None),
    )
    out_specs = (P("dp", "mp"), P("dp", "mp"), P("dp", "mp"), P("dp", "mp"))
    return jax.shard_map(
        on_device, mesh=mesh, in_specs=in_specs, out_specs=out_specs, check_vma=False
    )
```
